32 devices in a mesh: dp: 4 (over y, x), expert: 8 (over z, core).
Axes of the slice: x: 2, y: 2, z: 4, core: 2. Of those that a mesh axis runs over, the one named last changes fastest.
Arguments:
- tokens: bfloat16 [4096, 4096], P(('dp', 'expert')), may hold values from -6 to 6
- out_grad: bfloat16 [4096, 4096], P(('dp', 'expert')), may hold values from -0.75 to 0.75
- routes: int32 [4096, 1], P(('dp', 'expert')), may hold values from 0 to 7; in each aligned block of 128 rows (0 to 127, 128 to 255, ...) at most 24 rows name the same one
- gate_probs: bfloat16 [4096, 1], P(('dp', 'expert')), may hold values from 0.049804688 to 1
- w_gate: bfloat16 [8, 4096, 768], P('expert', None, 'dp'), may hold values from -0.09375 to 0.09375
- w_up: bfloat16 [8, 4096, 768], P('expert', None, 'dp'), may hold values from -0.09375 to 0.09375
- w_down: bfloat16 [8, 768, 4096], P('expert', 'dp'), may hold values from -0.21875 to 0.21875
Outputs:
- grad_tokens: bfloat16 [4096, 4096], P(('dp', 'expert'))
- grad_probs: bfloat16 [4096, 1], P(('dp', 'expert'))
- grad_w_gate: bfloat16 [8, 4096, 768], P('expert', None, 'dp')
- grad_w_up: bfloat16 [8, 4096, 768], P('expert', None, 'dp')
- grad_w_down: bfloat16 [8, 768, 4096], P('expert', 'dp')
The draws below stay inside these ranges and needn't reach their ends.
Inputs may be any that keep to these rules, and one draw needn't show every extreme that they name: `routes`: the experts of one token are different. Among the 128 tokens of one device no expert is named more than 24 times, a bound that some block reaches.
All inputs are finite; a program needn't handle non-finite values.
Results may differ from the reference program's by a relative error of at most 0.018.
Values may be sent and summed in bfloat16 or wider, within the bound.
A program may use at most 128 MiB of HBM per device.

```python
import math
import jax
import jax.numpy as jnp
import numpy as np
from jax import lax

D = 4096
H = 768
TOP = 1
TOK_DEV = 128
EXPERTS = 8
TOKENS = 4096
CAP = 24
N_DP = 4


def shard_levels(own_key, extent, cuts, least, largest):
    gain, own = 1.0, jax.random.fold_in(own_key, 6)
    for axis_at, shards_of in cuts:
        heights = jnp.exp(jax.random.uniform(jax.random.fold_in(own, axis_at), (shards_of,), jnp.float32, least / len(cuts), largest / len(cuts)))
        gain = gain * jnp.repeat(heights, extent[axis_at] // shards_of).reshape([-1 if axis == axis_at else 1 for axis in range(len(extent))])
    return gain


def routed_block(key, own, number, rows, count, top, most, lean):
    ranking = jax.random.permutation(key, count)
    packed, usual = shares(count, rows * top, most, lean, True), shares(count, rows * top, most, lean, False)
    places = jnp.arange(count)

    def named(lengths, rotation):
        used = int((lengths > 0).sum())
        fixed = max(1, used // 4)
        shifted = fixed + (places - fixed + rotation * (used - fixed)) % max(1, count - fixed)
        return jnp.zeros((count,), jnp.int32).at[ranking[jnp.where(places < fixed, places, shifted)]].set(jnp.asarray(lengths, jnp.int32))

    lengths = jnp.where(number % 4 == 0, named(packed, number // 4), named(usual, number - number // 4 - 1))
    mixed = jax.random.permutation(jax.random.fold_in(own, 3), count)
    donor, receiver = mixed[0:count // 2 * 2:2], mixed[1:count // 2 * 2:2]
    slack = jnp.minimum(lengths[donor] - 1, most - lengths[receiver]) // 2
    slack = jnp.where((donor == ranking[0]) | (receiver == ranking[0]) | (lengths[receiver] == 0), 0, jnp.maximum(slack, 0))
    shifted = jax.random.randint(jax.random.fold_in(own, 4), (count // 2,), 0, 1 << 20) % (slack + 1)
    lengths = lengths.at[donor].add(-shifted).at[receiver].add(shifted)
    labels = jnp.searchsorted(jnp.cumsum(lengths), jnp.arange(rows * top), side="right").astype(jnp.int32)
    table = labels.reshape(top, rows).T
    table = table[jax.random.permutation(jax.random.fold_in(own, 1), rows)]
    rotation = jax.random.randint(jax.random.fold_in(own, 2), (rows, 1), 0, top)
    return jnp.take_along_axis(table, (jnp.arange(top)[None, :] + rotation) % top, axis=1)


def shares(amount, total, limit, lean, full):
    weights = [(1 << 20) // math.isqrt(standing ** lean) + 1 for standing in range(1, amount + 1)]
    largest = limit if full else min(limit, max(-(-total // amount), total * weights[0] // sum(weights)))
    least = 1 if total - largest >= amount - 1 else 0
    holding, rest = [largest] + [least] * (amount - 1), total - largest - least * (amount - 1)
    while rest > 0:
        movable = [i for i in range(1, amount) if holding[i] < largest] or [i for i in range(1, amount) if holding[i] < limit]
        whole, remaining = sum([weights[i] for i in movable]), rest
        for i in movable:
            more = min(limit - holding[i], max(1, remaining * weights[i] // whole), rest)
            holding[i] = holding[i] + more
            rest = rest - more
    return np.array(holding)


def noise(rng, dims, width, limit, cuts=(), held_as=jnp.bfloat16):
    loudness = shard_levels(rng, dims, cuts, -0.22, 0.18) if cuts else 1.0
    values = jax.random.normal(rng, dims, jnp.float32) * width * loudness
    return jnp.minimum(jnp.maximum(values, -limit), limit).astype(held_as)


def setup_inputs(seed: int = 0) -> dict:
    key_list = jax.random.split(jax.random.key(seed), 8)
    tokens = noise(key_list[0], (TOKENS, D), 1.0, 6.0, ((0, 32),))
    out_grad = noise(key_list[1], (TOKENS, D), 0.125, 0.75, ((0, 32),))
    routes_keys = jax.random.split(jax.random.fold_in(key_list[2], 1), TOKENS // TOK_DEV)
    routes_turns = jax.random.permutation(jax.random.fold_in(key_list[2], 3), TOKENS // TOK_DEV)
    routes = jax.vmap(lambda own, number: routed_block(jax.random.fold_in(key_list[2], 2), own, number, TOK_DEV, EXPERTS, TOP, CAP, 2))(routes_keys, routes_turns).reshape((TOKENS, TOP))
    gate_probs = jnp.clip(0.049804688 + 0.9501953 * jax.random.uniform(key_list[3], (TOKENS, TOP), jnp.float32) ** shard_levels(key_list[3], (TOKENS, TOP), ((0, 32),), -0.2, 0.2), 0.049804688, 1.0).astype(jnp.bfloat16)
    w_gate = noise(key_list[4], (EXPERTS, D, H), D ** -0.5, 0.09375, ((0, 8), (2, 4)))
    w_up = noise(key_list[5], (EXPERTS, D, H), D ** -0.5, 0.09375, ((0, 8), (2, 4)))
    w_down = noise(key_list[6], (EXPERTS, H, D), H ** -0.5, 0.21875, ((0, 8), (1, 4)))
    return dict(tokens=tokens, out_grad=out_grad, routes=routes, gate_probs=gate_probs, w_gate=w_gate, w_up=w_up, w_down=w_down)


def expert_grads(pieces):
    rows_in, rows_dy, rows_prob, gate_w, up_w, down_w = pieces
    gate_pre = jnp.dot(rows_in, gate_w, preferred_element_type=jnp.float32)
    up_pre = jnp.dot(rows_in, up_w, preferred_element_type=jnp.float32)
    sigmoid_gate = jax.nn.sigmoid(gate_pre)
    active = gate_pre * sigmoid_gate
    hidden = (active * up_pre).astype(jnp.bfloat16)
    back_raw = jnp.dot(rows_dy, down_w.T, preferred_element_type=jnp.float32)
    scores = jnp.sum(back_raw * hidden.astype(jnp.float32), axis=1)
    weight_col = rows_prob.astype(jnp.float32)[:, None]
    scaled = (weight_col * rows_dy.astype(jnp.float32)).astype(jnp.bfloat16)
    grad_down = jnp.dot(hidden.T, scaled, preferred_element_type=jnp.float32).astype(jnp.bfloat16)
    back_hidden = weight_col * back_raw
    grad_gate_pre = (back_hidden * up_pre * sigmoid_gate * (1.0 + gate_pre * (1.0 - sigmoid_gate))).astype(jnp.bfloat16)
    grad_up_pre = (back_hidden * active).astype(jnp.bfloat16)
    grad_gate = jnp.dot(rows_in.T, grad_gate_pre, preferred_element_type=jnp.float32).astype(jnp.bfloat16)
    grad_up = jnp.dot(rows_in.T, grad_up_pre, preferred_element_type=jnp.float32).astype(jnp.bfloat16)
    block_width = H // N_DP
    summed = jnp.zeros((rows_in.shape[0], D), jnp.float32)
    for quarter in range(N_DP):
        start_col = quarter * block_width
        stop_col = start_col + block_width
        block_sum = jnp.dot(grad_gate_pre[:, start_col:stop_col], gate_w[:, start_col:stop_col].T, preferred_element_type=jnp.float32)
        block_sum = block_sum + jnp.dot(grad_up_pre[:, start_col:stop_col], up_w[:, start_col:stop_col].T, preferred_element_type=jnp.float32)
        rounded = lax.optimization_barrier(block_sum.astype(jnp.bfloat16))
        summed = summed + rounded.astype(jnp.float32)
    return summed.astype(jnp.bfloat16), scores.astype(jnp.bfloat16), grad_gate, grad_up, grad_down


def reference(tokens, out_grad, routes, gate_probs, w_gate, w_up, w_down):
    one_hot = (routes[:, :, None] == jnp.arange(EXPERTS, dtype=jnp.int32)[None, None, :]).astype(jnp.int32)
    blocked = one_hot.reshape(TOKENS // TOK_DEV, TOK_DEV * TOP, EXPERTS)
    earlier = jnp.cumsum(blocked, axis=1) - blocked
    slot_index = jnp.sum(earlier * blocked, axis=2).reshape(TOKENS, TOP).astype(jnp.int32)
    block_index = (jnp.arange(TOKENS, dtype=jnp.int32) // TOK_DEV)[:, None]
    row_index = (block_index * CAP + slot_index).astype(jnp.int32)
    row_count = (TOKENS // TOK_DEV) * CAP
    spread_in = jnp.broadcast_to(tokens[:, None, :], (TOKENS, TOP, D))
    spread_dy = jnp.broadcast_to(out_grad[:, None, :], (TOKENS, TOP, D))
    rows_in = jnp.zeros((EXPERTS, row_count, D), jnp.bfloat16).at[routes, row_index].set(spread_in)
    rows_dy = jnp.zeros((EXPERTS, row_count, D), jnp.bfloat16).at[routes, row_index].set(spread_dy)
    rows_prob = jnp.zeros((EXPERTS, row_count), jnp.bfloat16).at[routes, row_index].set(gate_probs)
    grad_rows, scores, grad_gate, grad_up, grad_down = lax.map(expert_grads, (rows_in, rows_dy, rows_prob, w_gate, w_up, w_down))
    picked = grad_rows[routes, row_index]
    grad_tokens = jnp.sum(picked.astype(jnp.float32), axis=1).astype(jnp.bfloat16)
    grad_probs = scores[routes, row_index]
    return grad_tokens, grad_probs, grad_gate, grad_up, grad_down
```

```python
import functools

import jax
import jax.numpy as jnp
from jax import lax
from jax.experimental import pallas as pl
from jax.experimental.pallas import tpu as pltpu
from jax.sharding import PartitionSpec as P

MESH = pl.DeviceIdType.MESH
LANES = 128
VMEM_LIMIT = 56 * 1024 * 1024


def partner(own, step, count):
    if count & (count - 1):
        return lax.rem(step - own + count, count)
    peer, bit = 0, 1
    while bit < count:
        mine, other = (own // bit) % 2, (step // bit) % 2
        peer = peer + bit * (mine + other - 2 * mine * other)
        bit *= 2
    return peer


def ring_places():
    own = lax.axis_index("dp")
    right = (2 * own + 1) % 5
    return own, right, 3 - right


def greet(count, own_e, right, left):
    barrier = pltpu.get_barrier_semaphore()
    for peer in (right, left):
        pl.semaphore_signal(barrier, inc=1, device_id={"dp": peer}, device_id_type=MESH)

    def step(k, carry):
        pl.semaphore_signal(
            barrier,
            inc=1,
            device_id={"expert": lax.rem(own_e + k, count)},
            device_id_type=MESH,
        )
        return carry

    lax.fori_loop(1, count, step, 0)
    pl.semaphore_wait(barrier, count + 1)


def remote(src, dst, send, recv, axis, peer):
    return pltpu.make_async_remote_copy(
        src_ref=src,
        dst_ref=dst,
        send_sem=send,
        recv_sem=recv,
        device_id={axis: peer},
        device_id_type=MESH,
    )


def spread_kernel(count, sent_in, sent_dy, all_in, all_dy, z_s, z_r, side_s, side_r, far_s, far_r, own_sem):
    own_e = lax.axis_index("expert")
    own_d, right, left = ring_places()
    sent, full = (sent_in, sent_dy), (all_in, all_dy)
    sides = (right, left)

    def z_copy(a, i):
        peer = partner(own_e, i, count)
        return remote(
            sent[a].at[peer], full[a].at[own_d, own_e], z_s.at[a, i], z_r.at[a, i], "expert", peer
        )

    def z_landed(a, i):
        place = full[a].at[own_d, partner(own_e, i, count)]
        return remote(place, place, z_s.at[a, i], z_r.at[a, i], "expert", own_e)

    def side_copy(a, way, i, src=None):
        place = full[a].at[own_d, partner(own_e, i, count)]
        return remote(
            place if src is None else src, place, side_s.at[a, way, i], side_r.at[a, way, i], "dp", sides[way]
        )

    def side_landed(a, way, i):
        place = full[a].at[sides[1 - way], partner(own_e, i, count)]
        return remote(place, place, side_s.at[a, way, i], side_r.at[a, way, i], "dp", sides[way])

    def far_copy(a, i):
        place = full[a].at[sides[1 - a], partner(own_e, i, count)]
        return remote(place, place, far_s.at[a, i], far_r.at[a, i], "dp", sides[a])

    def far_landed(a, i):
        place = full[a].at[3 - own_d, partner(own_e, i, count)]
        return remote(place, place, far_s.at[a, i], far_r.at[a, i], "dp", sides[a])

    own = [
        pltpu.make_async_copy(sent[a].at[own_e], full[a].at[own_d, own_e], own_sem.at[a])
        for a in range(2)
    ]
    for a in range(2):
        own[a].start()
    greet(count, own_e, right, left)
    for a in range(2):
        for way in range(2):
            side_copy(a, way, 0, sent[a].at[own_e]).start()

    def start(i, carry):
        for a in range(2):
            z_copy(a, i).start()
        return carry

    lax.fori_loop(1, count, start, 0)

    def onward(i):
        for a in range(2):
            side_landed(a, a, i).wait_recv()
            far_copy(a, i).start()

    def relay(i, carry):
        for a in range(2):
            z_landed(a, i).wait_recv()
            for way in range(2):
                side_copy(a, way, i).start()
        onward(i - 1)
        return carry

    lax.fori_loop(1, count, relay, 0)
    onward(count - 1)

    def finish(i, carry):
        for a in range(2):
            side_landed(a, 1 - a, i).wait_recv()
            far_landed(a, i).wait_recv()
            far_copy(a, i).wait_send()
            for way in range(2):
                side_copy(a, way, i).wait_send()
        return carry

    lax.fori_loop(0, count, finish, 0)

    def sent_off(i, carry):
        for a in range(2):
            z_copy(a, i).wait_send()
        return carry

    lax.fori_loop(1, count, sent_off, 0)
    for a in range(2):
        own[a].wait()


def spread(sent_in, sent_dy, dp_count):
    count = sent_in.shape[0]
    shape = jax.ShapeDtypeStruct((dp_count,) + sent_in.shape, sent_in.dtype)
    dma = pltpu.SemaphoreType.DMA
    return pl.pallas_call(
        functools.partial(spread_kernel, count),
        out_shape=(shape, shape),
        in_specs=[pl.BlockSpec(memory_space=pl.ANY)] * 2,
        out_specs=[pl.BlockSpec(memory_space=pl.ANY)] * 2,
        scratch_shapes=[
            dma((2, count)),
            dma((2, count)),
            dma((2, 2, count)),
            dma((2, 2, count)),
            dma((2, count)),
            dma((2, count)),
            dma((2,)),
        ],
        compiler_params=pltpu.CompilerParams(
            collective_id=0, has_side_effects=True, vmem_limit_bytes=VMEM_LIMIT
        ),
        name="spread",
    )(sent_in, sent_dy)


def col_tiles(first, last, width):
    while first < last:
        yield slice(first, min(first + width, last))
        first = min(first + width, last)


def gather_kernel(
    count, chunks, gg, gu, score, gate_w, up_w, back, part, far_l, far_r, near_l, near_r, zed,
    far_s, far_rs, side_s, side_rs, sum_s, sum_rs, z_s, z_r, own_sem,
):
    own_e = lax.axis_index("expert")
    own_d, right, left = ring_places()
    width = gate_w.shape[0]
    rows = part.shape[1]
    cols = part.shape[2]
    cap = rows // count
    step_rows = rows // chunks
    slabs = count // chunks
    half = width // 2
    halves = (pl.ds(0, half), pl.ds(half, cols - half))
    spans = ((0, half), (half, cols))
    sides = (right, left)
    far_in = (far_l, far_r)
    near_in = (near_l, near_r)
    targets = (right, left, 3 - own_d, own_d)
    tile = 512

    def rows_at(c):
        return pl.ds(pl.multiple_of(c * step_rows, step_rows), step_rows)

    def far_copy(way, c):
        return remote(
            part.at[2, rows_at(c), halves[way]], far_in[way].at[rows_at(c)],
            far_s.at[way, c], far_rs.at[way, c], "dp", sides[way],
        )

    def side_copy(way, c):
        return remote(
            part.at[way, rows_at(c), halves[1 - way]], near_in[way].at[rows_at(c), halves[1 - way]],
            side_s.at[way, c], side_rs.at[way, c], "dp", sides[way],
        )

    def sum_copy(way, c):
        return remote(
            part.at[way, rows_at(c), halves[way]], near_in[way].at[rows_at(c), halves[way]],
            sum_s.at[way, c], sum_rs.at[way, c], "dp", sides[way],
        )

    def compute(slot):
        row0 = pl.multiple_of(targets[slot] * rows, rows)
        g = gg[pl.ds(row0, rows), :]
        u = gu[pl.ds(row0, rows), :]
        part[slot, :, width:cols] = score[pl.ds(row0, rows), :]

        def one(j, carry):
            at = pl.ds(pl.multiple_of(j * tile, tile), tile)
            dims = (((1,), (1,)), ((), ()))
            value = lax.dot_general(g, gate_w[at, :], dims, preferred_element_type=jnp.float32)
            value = value + lax.dot_general(u, up_w[at, :], dims, preferred_element_type=jnp.float32)
            part[slot, :, at] = value.astype(part.dtype)
            return carry

        lax.fori_loop(0, width // tile, one, 0)

    def for_chunks(f):
        def go(c, carry):
            f(c)
            return carry

        lax.fori_loop(0, chunks, go, 0)

    greet(count, own_e, right, left)
    compute(2)

    @for_chunks
    def _(c):
        for way in range(2):
            far_copy(way, c).start()

    for way in range(2):
        compute(way)

        @for_chunks
        def _(c):
            side_copy(way, c).start()

    compute(3)

    @for_chunks
    def _(c):
        for way in range(2):
            far_copy(way, c).wait_recv()
            for at in col_tiles(*spans[way], tile):
                there = slice(at.start - spans[way][0], at.stop - spans[way][0])
                total = part[way, rows_at(c), at].astype(jnp.float32) + far_in[way][
                    rows_at(c), there
                ].astype(jnp.float32)
                part[way, rows_at(c), at] = total.astype(part.dtype)
            sum_copy(way, c).start()

    def z_copy(i):
        peer = partner(own_e, i, count)
        return remote(zed.at[peer], back.at[own_e], z_s.at[i], z_r.at[i], "expert", peer)

    def z_landed(i):
        place = back.at[partner(own_e, i, count)]
        return remote(place, place, z_s.at[i], z_r.at[i], "expert", own_e)

    def merge(c):
        for way in range(2):
            side_copy(way, c).wait_recv()
            sum_copy(way, c).wait_recv()
        for at in col_tiles(0, cols, tile):
            total = part[3, rows_at(c), at].astype(jnp.float32)
            total = total + near_l[rows_at(c), at].astype(jnp.float32)
            total = total + near_r[rows_at(c), at].astype(jnp.float32)
            total = total.reshape(slabs, cap, at.stop - at.start)
            zed[pl.ds(c * slabs, slabs), :, at] = total.astype(zed.dtype)

    @for_chunks
    def _(c):
        merge(c)
        for k in range(slabs):
            there = c * slabs + k
            step = partner(own_e, there, count)

            @pl.when(there != own_e)
            def _():
                z_copy(step).start()

    own = pltpu.make_async_copy(zed.at[own_e], back.at[own_e], own_sem.at[0])
    own.start()
    own.wait()

    def landed(i, carry):
        z_landed(i).wait_recv()
        z_copy(i).wait_send()
        return carry

    lax.fori_loop(1, count, landed, 0)

    @for_chunks
    def _(c):
        for way in range(2):
            far_copy(way, c).wait_send()
            side_copy(way, c).wait_send()
            sum_copy(way, c).wait_send()


def gather(gg, gu, score, gate_w, up_w, count, dp_count):
    width = gate_w.shape[0]
    rows = gg.shape[0] // dp_count
    cols = width + LANES
    half = width // 2
    chunks = 4 if count % 4 == 0 and (rows // 4) % 16 == 0 else 1
    dma = pltpu.SemaphoreType.DMA
    kind = jnp.bfloat16
    pairs = dma((2, chunks))
    return pl.pallas_call(
        functools.partial(gather_kernel, count, chunks),
        out_shape=jax.ShapeDtypeStruct((count, rows // count, cols), kind),
        in_specs=[pl.BlockSpec(memory_space=pltpu.VMEM)] * 5,
        out_specs=pl.BlockSpec(memory_space=pl.ANY),
        scratch_shapes=[
            pltpu.VMEM((4, rows, cols), kind),
            pltpu.VMEM((rows, half), kind),
            pltpu.VMEM((rows, cols - half), kind),
            pltpu.VMEM((rows, cols), kind),
            pltpu.VMEM((rows, cols), kind),
            pltpu.VMEM((count, rows // count, cols), kind),
            pairs,
            pairs,
            pairs,
            pairs,
            pairs,
            pairs,
            dma((count,)),
            dma((count,)),
            dma((1,)),
        ],
        compiler_params=pltpu.CompilerParams(
            collective_id=1, has_side_effects=True, vmem_limit_bytes=VMEM_LIMIT
        ),
        name="gather",
    )(gg, gu, score, gate_w, up_w)


def body(tokens, out_grad, routes, gate_probs, w_gate, w_up, w_down):
    expert_count = lax.axis_size("expert")
    dp_count = lax.axis_size("dp")
    tok_count, width = tokens.shape
    top_count = routes.shape[1]
    capacity = 3 * tok_count * top_count // (2 * expert_count)
    capacity = -(-capacity // 8) * 8
    slot_total = expert_count * capacity
    flat_routes = routes.reshape(-1)
    order = jnp.arange(flat_routes.shape[0], dtype=jnp.int32)
    same = (flat_routes[:, None] == flat_routes[None, :]) & (order[None, :] < order[:, None])
    slot_index = jnp.sum(same.astype(jnp.int32), axis=1)
    destination = flat_routes * capacity + slot_index
    placing = jnp.arange(slot_total, dtype=jnp.int32)[:, None] == destination[None, :]
    weights = gate_probs.reshape(-1).astype(jnp.float32)
    by_token = placing.astype(jnp.bfloat16).reshape(slot_total, tok_count, top_count)
    collect = jnp.sum(by_token, axis=2)
    weighted = jnp.where(placing, weights[None, :], 0.0).astype(jnp.bfloat16)
    collect_weighted = jnp.sum(weighted.reshape(slot_total, tok_count, top_count), axis=2)
    sent_shape = (expert_count, capacity, width)
    sent_in = (
        jnp.dot(collect, tokens, preferred_element_type=jnp.float32)
        .astype(jnp.bfloat16)
        .reshape(sent_shape)
    )
    sent_dy = (
        jnp.dot(collect_weighted, out_grad, preferred_element_type=jnp.float32)
        .astype(jnp.bfloat16)
        .reshape(sent_shape)
    )
    all_in, all_dy = spread(sent_in, sent_dy, dp_count)
    row_total = dp_count * slot_total
    rows_in = all_in.reshape(row_total, width)
    scaled = all_dy.reshape(row_total, width)
    gate_w = w_gate[0]
    up_w = w_up[0]
    down_w = w_down[0]
    contract_last = (((1,), (1,)), ((), ()))
    contract_first = (((0,), (0,)), ((), ()))
    gate_pre = jnp.dot(rows_in, gate_w, preferred_element_type=jnp.float32)
    up_pre = jnp.dot(rows_in, up_w, preferred_element_type=jnp.float32)
    sigmoid_gate = jax.nn.sigmoid(gate_pre)
    active = gate_pre * sigmoid_gate
    hidden = (active * up_pre).astype(jnp.bfloat16)
    back_hidden = lax.dot_general(scaled, down_w, contract_last, preferred_element_type=jnp.float32)
    grad_gate_pre = (
        back_hidden * up_pre * sigmoid_gate * (1.0 + gate_pre * (1.0 - sigmoid_gate))
    ).astype(jnp.bfloat16)
    grad_up_pre = (back_hidden * active).astype(jnp.bfloat16)
    score = jnp.sum(back_hidden * hidden.astype(jnp.float32), axis=1, keepdims=True)
    score = jnp.broadcast_to(score, (row_total, LANES)).astype(jnp.bfloat16)
    back = gather(grad_gate_pre, grad_up_pre, score, gate_w, up_w, expert_count, dp_count)
    grad_down = lax.dot_general(
        hidden, scaled, contract_first, preferred_element_type=jnp.float32
    ).astype(jnp.bfloat16)
    grad_gate = lax.dot_general(
        rows_in, grad_gate_pre, contract_first, preferred_element_type=jnp.float32
    ).astype(jnp.bfloat16)
    grad_up = lax.dot_general(
        rows_in, grad_up_pre, contract_first, preferred_element_type=jnp.float32
    ).astype(jnp.bfloat16)
    back = back.reshape(slot_total, width + LANES)
    grad_tokens = lax.dot_general(
        collect, back[:, :width], contract_first, preferred_element_type=jnp.float32
    ).astype(jnp.bfloat16)
    picked = lax.dot_general(
        placing.astype(jnp.bfloat16),
        back[:, width:],
        contract_first,
        preferred_element_type=jnp.float32,
    )[:, 0]
    grad_probs = (picked / weights).astype(jnp.bfloat16).reshape(tok_count, top_count)
    return (grad_tokens, grad_probs, grad_gate[None], grad_up[None], grad_down[None])


def solution(mesh):
    in_specs = (
        P(("dp", "expert"), None),
        P(("dp", "expert"), None),
        P(("dp", "expert"), None),
        P(("dp", "expert"), None),
        P("expert", None, "dp"),
        P("expert", None, "dp"),
        P("expert", "dp", None),
    )
    out_specs = (
        P(("dp", "expert"), None),
        P(("dp", "expert"), None),
        P("expert", None, "dp"),
        P("expert", None, "dp"),
        P("expert", "dp", None),
    )
    return jax.shard_map(body, mesh=mesh, in_specs=in_specs, out_specs=out_specs, check_vma=False)
```

```python
import functools

import jax
import jax.numpy as jnp
from jax import lax
from jax.experimental import pallas as pl
from jax.experimental.pallas import tpu as pltpu
from jax.sharding import PartitionSpec as P

MESH = pl.DeviceIdType.MESH
LANES = 128
VMEM_LIMIT = 60 * 1024 * 1024


def partner(own, step, count):
    if count & (count - 1):
        return lax.rem(step - own + count, count)
    peer, bit = 0, 1
    while bit < count:
        mine, other = (own // bit) % 2, (step // bit) % 2
        peer = peer + bit * (mine + other - 2 * mine * other)
        bit *= 2
    return peer


def ring_places():
    own = lax.axis_index("dp")
    right = (2 * own + 1) % 5
    return own, right, 3 - right


def greet(count, own_e, right, left):
    barrier = pltpu.get_barrier_semaphore()
    for peer in (right, left):
        pl.semaphore_signal(barrier, inc=1, device_id={"dp": peer}, device_id_type=MESH)

    def step(k, carry):
        pl.semaphore_signal(
            barrier,
            inc=1,
            device_id={"expert": lax.rem(own_e + k, count)},
            device_id_type=MESH,
        )
        return carry

    lax.fori_loop(1, count, step, 0)
    pl.semaphore_wait(barrier, count + 1)


def remote(src, dst, send, recv, axis, peer):
    return pltpu.make_async_remote_copy(
        src_ref=src,
        dst_ref=dst,
        send_sem=send,
        recv_sem=recv,
        device_id={axis: peer},
        device_id_type=MESH,
    )


def spread_kernel(count, sent_in, sent_dy, all_in, all_dy, z_s, z_r, side_s, side_r, far_s, far_r, own_sem):
    own_e = lax.axis_index("expert")
    own_d, right, left = ring_places()
    sent, full = (sent_in, sent_dy), (all_in, all_dy)
    sides = (right, left)

    def z_copy(a, i):
        peer = partner(own_e, i, count)
        return remote(
            sent[a].at[peer], full[a].at[own_d, own_e], z_s.at[a, i], z_r.at[a, i], "expert", peer
        )

    def z_landed(a, i):
        place = full[a].at[own_d, partner(own_e, i, count)]
        return remote(place, place, z_s.at[a, i], z_r.at[a, i], "expert", own_e)

    def side_copy(a, way, i, src=None):
        place = full[a].at[own_d, partner(own_e, i, count)]
        return remote(
            place if src is None else src, place, side_s.at[a, way, i], side_r.at[a, way, i], "dp", sides[way]
        )

    def side_landed(a, way, i):
        place = full[a].at[sides[1 - way], partner(own_e, i, count)]
        return remote(place, place, side_s.at[a, way, i], side_r.at[a, way, i], "dp", sides[way])

    def far_copy(a, i):
        place = full[a].at[sides[1 - a], partner(own_e, i, count)]
        return remote(place, place, far_s.at[a, i], far_r.at[a, i], "dp", sides[a])

    def far_landed(a, i):
        place = full[a].at[3 - own_d, partner(own_e, i, count)]
        return remote(place, place, far_s.at[a, i], far_r.at[a, i], "dp", sides[a])

    own = [
        pltpu.make_async_copy(sent[a].at[own_e], full[a].at[own_d, own_e], own_sem.at[a])
        for a in range(2)
    ]
    for a in range(2):
        own[a].start()
    greet(count, own_e, right, left)
    for a in range(2):
        for way in range(2):
            side_copy(a, way, 0, sent[a].at[own_e]).start()

    def start(i, carry):
        for a in range(2):
            z_copy(a, i).start()
        return carry

    lax.fori_loop(1, count, start, 0)

    def onward(i):
        for a in range(2):
            side_landed(a, a, i).wait_recv()
            far_copy(a, i).start()

    def relay(i, carry):
        for a in range(2):
            z_landed(a, i).wait_recv()
            for way in range(2):
                side_copy(a, way, i).start()
        onward(i - 1)
        return carry

    lax.fori_loop(1, count, relay, 0)
    onward(count - 1)

    def finish(i, carry):
        for a in range(2):
            side_landed(a, 1 - a, i).wait_recv()
            far_landed(a, i).wait_recv()
            far_copy(a, i).wait_send()
            for way in range(2):
                side_copy(a, way, i).wait_send()
        return carry

    lax.fori_loop(0, count, finish, 0)

    def sent_off(i, carry):
        for a in range(2):
            z_copy(a, i).wait_send()
        return carry

    lax.fori_loop(1, count, sent_off, 0)
    for a in range(2):
        own[a].wait()


def spread(sent_in, sent_dy, dp_count):
    count = sent_in.shape[0]
    shape = jax.ShapeDtypeStruct((dp_count,) + sent_in.shape, sent_in.dtype)
    dma = pltpu.SemaphoreType.DMA
    return pl.pallas_call(
        functools.partial(spread_kernel, count),
        out_shape=(shape, shape),
        in_specs=[pl.BlockSpec(memory_space=pl.ANY)] * 2,
        out_specs=[pl.BlockSpec(memory_space=pl.ANY)] * 2,
        scratch_shapes=[
            dma((2, count)),
            dma((2, count)),
            dma((2, 2, count)),
            dma((2, 2, count)),
            dma((2, count)),
            dma((2, count)),
            dma((2,)),
        ],
        compiler_params=pltpu.CompilerParams(
            collective_id=0, has_side_effects=True, vmem_limit_bytes=VMEM_LIMIT
        ),
        name="spread",
    )(sent_in, sent_dy)


def col_tiles(first, last, width):
    while first < last:
        yield slice(first, min(first + width, last))
        first = min(first + width, last)


def gather_kernel(
    count, chunks, gg, gu, score, gate_w, up_w, back, part, far_l, far_r, near_l, near_r, zed,
    far_s, far_rs, side_s, side_rs, sum_s, sum_rs, z_s, z_r, own_sem,
):
    own_e = lax.axis_index("expert")
    own_d, right, left = ring_places()
    width = gate_w.shape[0]
    rows = part.shape[1]
    cols = part.shape[2]
    cap = rows // count
    step_rows = rows // chunks
    slabs = count // chunks
    half = width // 2
    halves = (pl.ds(0, half), pl.ds(half, cols - half))
    spans = ((0, half), (half, cols))
    sides = (right, left)
    far_in = (far_l, far_r)
    near_in = (near_l, near_r)
    targets = (right, left, 3 - own_d, own_d)
    tile = 512

    def rows_at(c):
        return pl.ds(pl.multiple_of(c * step_rows, step_rows), step_rows)

    def far_copy(way, c):
        return remote(
            part.at[2, rows_at(c), halves[way]], far_in[way].at[rows_at(c)],
            far_s.at[way, c], far_rs.at[way, c], "dp", sides[way],
        )

    def side_copy(way, c):
        return remote(
            part.at[way, rows_at(c), halves[1 - way]], near_in[way].at[rows_at(c), halves[1 - way]],
            side_s.at[way, c], side_rs.at[way, c], "dp", sides[way],
        )

    def sum_copy(way, c):
        return remote(
            part.at[way, rows_at(c), halves[way]], near_in[way].at[rows_at(c), halves[way]],
            sum_s.at[way, c], sum_rs.at[way, c], "dp", sides[way],
        )

    def compute(slot):
        row0 = pl.multiple_of(targets[slot] * rows, rows)
        g = gg[pl.ds(row0, rows), :]
        u = gu[pl.ds(row0, rows), :]
        part[slot, :, width:cols] = score[pl.ds(row0, rows), :]

        def one(j, carry):
            at = pl.ds(pl.multiple_of(j * tile, tile), tile)
            dims = (((1,), (1,)), ((), ()))
            value = lax.dot_general(g, gate_w[at, :], dims, preferred_element_type=jnp.float32)
            value = value + lax.dot_general(u, up_w[at, :], dims, preferred_element_type=jnp.float32)
            part[slot, :, at] = value.astype(part.dtype)
            return carry

        lax.fori_loop(0, width // tile, one, 0)

    def for_chunks(f):
        def go(c, carry):
            f(c)
            return carry

        lax.fori_loop(0, chunks, go, 0)

    greet(count, own_e, right, left)
    compute(2)

    @for_chunks
    def _(c):
        for way in range(2):
            far_copy(way, c).start()

    for way in range(2):
        compute(way)

        @for_chunks
        def _(c):
            side_copy(way, c).start()

    compute(3)

    @for_chunks
    def _(c):
        for way in range(2):
            far_copy(way, c).wait_recv()
            for at in col_tiles(*spans[way], tile):
                there = slice(at.start - spans[way][0], at.stop - spans[way][0])
                total = part[way, rows_at(c), at].astype(jnp.float32) + far_in[way][
                    rows_at(c), there
                ].astype(jnp.float32)
                part[way, rows_at(c), at] = total.astype(part.dtype)
            sum_copy(way, c).start()

    def z_copy(i):
        peer = partner(own_e, i, count)
        return remote(zed.at[peer], back.at[own_e], z_s.at[i], z_r.at[i], "expert", peer)

    def z_landed(i):
        place = back.at[partner(own_e, i, count)]
        return remote(place, place, z_s.at[i], z_r.at[i], "expert", own_e)

    def merge(c):
        for way in range(2):
            side_copy(way, c).wait_recv()
            sum_copy(way, c).wait_recv()
        for at in col_tiles(0, cols, tile):
            total = part[3, rows_at(c), at].astype(jnp.float32)
            total = total + near_l[rows_at(c), at].astype(jnp.float32)
            total = total + near_r[rows_at(c), at].astype(jnp.float32)
            total = total.reshape(slabs, cap, at.stop - at.start)
            zed[pl.ds(c * slabs, slabs), :, at] = total.astype(zed.dtype)

    @for_chunks
    def _(c):
        merge(c)
        for k in range(slabs):
            there = c * slabs + k
            step = partner(own_e, there, count)

            @pl.when(there != own_e)
            def _():
                z_copy(step).start()

    own = pltpu.make_async_copy(zed.at[own_e], back.at[own_e], own_sem.at[0])
    own.start()
    own.wait()

    def landed(i, carry):
        z_landed(i).wait_recv()
        z_copy(i).wait_send()
        return carry

    lax.fori_loop(1, count, landed, 0)

    @for_chunks
    def _(c):
        for way in range(2):
            far_copy(way, c).wait_send()
            side_copy(way, c).wait_send()
            sum_copy(way, c).wait_send()


def gather(gg, gu, score, gate_w, up_w, count, dp_count):
    width = gate_w.shape[0]
    rows = gg.shape[0] // dp_count
    cols = width + LANES
    half = width // 2
    chunks = 4 if count % 4 == 0 and (rows // 4) % 16 == 0 else 1
    dma = pltpu.SemaphoreType.DMA
    kind = jnp.bfloat16
    pairs = dma((2, chunks))
    return pl.pallas_call(
        functools.partial(gather_kernel, count, chunks),
        out_shape=jax.ShapeDtypeStruct((count, rows // count, cols), kind),
        in_specs=[pl.BlockSpec(memory_space=pltpu.VMEM)] * 5,
        out_specs=pl.BlockSpec(memory_space=pl.ANY),
        scratch_shapes=[
            pltpu.VMEM((4, rows, cols), kind),
            pltpu.VMEM((rows, half), kind),
            pltpu.VMEM((rows, cols - half), kind),
            pltpu.VMEM((rows, cols), kind),
            pltpu.VMEM((rows, cols), kind),
            pltpu.VMEM((count, rows // count, cols), kind),
            pairs,
            pairs,
            pairs,
            pairs,
            pairs,
            pairs,
            dma((count,)),
            dma((count,)),
            dma((1,)),
        ],
        compiler_params=pltpu.CompilerParams(
            collective_id=1, has_side_effects=True, vmem_limit_bytes=VMEM_LIMIT
        ),
        name="gather",
    )(gg, gu, score, gate_w, up_w)


def fused_kernel(
    count, sent_in, sent_dy, gate_w, up_w, down_w,
    all_in, all_dy, back, grad_gate, grad_up, grad_down,
    stage, flat_in, flat_dy, hid, dgate, dup, part, far_l, far_r, near_l, near_r, zed,
    z_s, z_r, side_s, side_r, far_s, far_r_sem, own_sem, stage_sem,
    rf_s, rf_r, rd_s, rd_r, rs_s, rs_r, home_s, home_r,
):
    own_e = lax.axis_index("expert")
    own_d, right, left = ring_places()
    sent, full, flat = (sent_in, sent_dy), (all_in, all_dy), (flat_in, flat_dy)
    sides = (right, left)
    dp_count, _, cap, width = all_in.shape
    cols = part.shape[3]
    group = dp_count * cap
    half = width // 2
    halves = (pl.ds(0, half), pl.ds(half, cols - half))
    spans = ((0, half), (half, cols))
    far_in, near_in = (far_l, far_r), (near_l, near_r)
    tile = 512
    last_dims = (((1,), (1,)), ((), ()))
    first_dims = (((0,), (0,)), ((), ()))

    def z_copy(a, i):
        peer = partner(own_e, i, count)
        return remote(
            sent[a].at[peer], full[a].at[own_d, own_e], z_s.at[a, i], z_r.at[a, i], "expert", peer
        )

    def z_landed(a, i):
        place = full[a].at[own_d, partner(own_e, i, count)]
        return remote(place, place, z_s.at[a, i], z_r.at[a, i], "expert", own_e)

    def side_copy(a, way, i, src=None):
        place = full[a].at[own_d, partner(own_e, i, count)]
        return remote(
            place if src is None else src, place, side_s.at[a, way, i], side_r.at[a, way, i], "dp", sides[way]
        )

    def side_landed(a, way, i):
        place = full[a].at[sides[1 - way], partner(own_e, i, count)]
        return remote(place, place, side_s.at[a, way, i], side_r.at[a, way, i], "dp", sides[way])

    def onward_copy(a, i):
        place = full[a].at[sides[1 - a], partner(own_e, i, count)]
        return remote(place, place, far_s.at[a, i], far_r_sem.at[a, i], "dp", sides[a])

    def onward_landed(a, i):
        place = full[a].at[3 - own_d, partner(own_e, i, count)]
        return remote(place, place, far_s.at[a, i], far_r_sem.at[a, i], "dp", sides[a])

    def rf_copy(way, c):
        return remote(
            part.at[3 - own_d, c, :, halves[way]], far_in[way].at[c],
            rf_s.at[way, c], rf_r.at[way, c], "dp", sides[way],
        )

    def rd_copy(way, c):
        return remote(
            part.at[sides[way], c, :, halves[1 - way]], near_in[way].at[c, :, halves[1 - way]],
            rd_s.at[way, c], rd_r.at[way, c], "dp", sides[way],
        )

    def rs_copy(way, c):
        return remote(
            part.at[sides[way], c, :, halves[way]], near_in[way].at[c, :, halves[way]],
            rs_s.at[way, c], rs_r.at[way, c], "dp", sides[way],
        )

    def home_copy(i):
        peer = partner(own_e, i, count)
        return remote(zed.at[i], back.at[own_e], home_s.at[i], home_r.at[i], "expert", peer)

    def home_landed(i):
        place = back.at[partner(own_e, i, count)]
        return remote(place, place, home_s.at[i], home_r.at[i], "expert", own_e)

    own = [
        pltpu.make_async_copy(sent[a].at[own_e], full[a].at[own_d, own_e], own_sem.at[a])
        for a in range(2)
    ]
    for a in range(2):
        own[a].start()
    greet(count, own_e, right, left)
    for a in range(2):
        for way in range(2):
            side_copy(a, way, 0, sent[a].at[own_e]).start()

    def start(i, carry):
        for a in range(2):
            z_copy(a, i).start()
        return carry

    lax.fori_loop(1, count, start, 0)
    for a in range(2):
        own[a].wait()

    def relay(i):
        for a in range(2):
            z_landed(a, i).wait_recv()
            for way in range(2):
                side_copy(a, way, i).start()

    def onward(i):
        for a in range(2):
            side_landed(a, a, i).wait_recv()
            onward_copy(a, i).start()

    def compute(i):
        src = partner(own_e, i, count)
        for a in range(2):
            side_landed(a, 1 - a, i).wait_recv()
            onward_landed(a, i).wait_recv()
        loads = [
            pltpu.make_async_copy(full[a].at[:, src], stage.at[a], stage_sem.at[a])
            for a in range(2)
        ]
        for load in loads:
            load.start()
        for load in loads:
            load.wait()
        rows = pl.ds(pl.multiple_of(i * group, group), group)
        for a in range(2):
            for at in col_tiles(0, width, tile):
                value = stage[a, :, :, at].astype(jnp.float32).reshape(group, tile)
                flat[a][rows, at] = value.astype(flat[a].dtype)

        def product(x, w):
            return lax.dot_general(x, w, last_dims, preferred_element_type=jnp.float32)

        gate_pre = product(flat_in[rows, :], gate_w[...])
        up_pre = product(flat_in[rows, :], up_w[...])
        back_hidden = product(flat_dy[rows, :], down_w[...])
        sigmoid_gate = jax.nn.sigmoid(gate_pre)
        active = gate_pre * sigmoid_gate
        hidden = (active * up_pre).astype(jnp.bfloat16)
        score = jnp.sum(back_hidden * hidden.astype(jnp.float32), axis=1, keepdims=True)
        g = (back_hidden * up_pre * sigmoid_gate * (1.0 + gate_pre * (1.0 - sigmoid_gate))).astype(
            jnp.bfloat16
        )
        u = (back_hidden * active).astype(jnp.bfloat16)
        hid[rows, :] = hidden
        dgate[rows, :] = g
        dup[rows, :] = u
        score = jnp.broadcast_to(score, (group, cols - width)).reshape(dp_count, cap, cols - width)
        part[:, i, :, width:cols] = score.astype(part.dtype)
        for at in col_tiles(0, width, tile):
            value = jnp.dot(g, gate_w[:, at], preferred_element_type=jnp.float32)
            value = value + jnp.dot(u, up_w[:, at], preferred_element_type=jnp.float32)
            part[:, i, :, at] = value.reshape(dp_count, cap, tile).astype(part.dtype)
        for way in range(2):
            rf_copy(way, i).start()
        for way in range(2):
            rd_copy(way, i).start()

    def ring_sum(i):
        for way in range(2):
            rf_copy(way, i).wait_recv()
            for at in col_tiles(*spans[way], tile):
                there = slice(at.start - spans[way][0], at.stop - spans[way][0])
                total = part[sides[way], i, :, at].astype(jnp.float32)
                total = total + far_in[way][i, :, there].astype(jnp.float32)
                part[sides[way], i, :, at] = total.astype(part.dtype)
            rs_copy(way, i).start()

    def merge(i):
        for way in range(2):
            rd_copy(way, i).wait_recv()
            rs_copy(way, i).wait_recv()
        for at in col_tiles(0, cols, tile):
            total = part[own_d, i, :, at].astype(jnp.float32)
            total = total + near_l[i, :, at].astype(jnp.float32)
            total = total + near_r[i, :, at].astype(jnp.float32)
            zed[i, :, at] = total.astype(zed.dtype)

        @pl.when(i > 0)
        def _():
            home_copy(i).start()

    def weight_grad(out, left_rows, right_rows):
        def one(j, carry):
            at = pl.ds(pl.multiple_of(j * tile, tile), tile)
            value = lax.dot_general(
                left_rows[...], right_rows[:, at], first_dims, preferred_element_type=jnp.float32
            )
            out[:, at] = value.astype(out.dtype)
            return carry

        lax.fori_loop(0, width // tile, one, 0)

    grads = ((grad_down, hid, flat_dy), (grad_gate, dgate, flat_in), (grad_up, dup, flat_in))

    def step(t, carry):
        def during(lag, first, f):
            @pl.when((t - lag >= first) & (t - lag < count))
            def _():
                f(t - lag)

        during(0, 1, relay)
        during(1, 0, onward)
        during(3, 0, ring_sum)
        during(2, 0, compute)
        during(4, 0, merge)
        for k, grad in enumerate(grads):
            @pl.when(t == count + 2 + (k + 1) // 2)
            def _():
                weight_grad(*grad)

        return carry

    lax.fori_loop(0, count + 4, step, 0)
    keep = pltpu.make_async_copy(zed.at[0], back.at[own_e], own_sem.at[0])
    keep.start()
    keep.wait()

    def finish(i, carry):
        for a in range(2):
            onward_copy(a, i).wait_send()
            for way in range(2):
                side_copy(a, way, i).wait_send()
        for way in range(2):
            rf_copy(way, i).wait_send()
            rd_copy(way, i).wait_send()
            rs_copy(way, i).wait_send()
        return carry

    lax.fori_loop(0, count, finish, 0)

    def landed(i, carry):
        for a in range(2):
            z_copy(a, i).wait_send()
        home_landed(i).wait_recv()
        home_copy(i).wait_send()
        return carry

    lax.fori_loop(1, count, landed, 0)


def fused(sent_in, sent_dy, gate_t, up_t, down_w, dp_count):
    count, cap, width = sent_in.shape
    kind = sent_in.dtype
    hidden = down_w.shape[0]
    cols, half = width + LANES, width // 2
    total = dp_count * count * cap
    dma = pltpu.SemaphoreType.DMA
    full = jax.ShapeDtypeStruct((dp_count, count, cap, width), kind)
    grad = jax.ShapeDtypeStruct((hidden, width), kind)
    whole = pl.BlockSpec(memory_space=pltpu.VMEM)
    apart = pl.BlockSpec(memory_space=pl.ANY)
    pair = dma((2, count))
    results = pl.pallas_call(
        functools.partial(fused_kernel, count),
        out_shape=(full, full, jax.ShapeDtypeStruct((count, cap, cols), kind), grad, grad, grad),
        in_specs=[apart, apart, whole, whole, whole],
        out_specs=[apart, apart, apart, whole, whole, whole],
        scratch_shapes=[
            pltpu.VMEM((2, dp_count, cap, width), kind),
            pltpu.VMEM((total, width), kind),
            pltpu.VMEM((total, width), kind),
            pltpu.VMEM((total, hidden), kind),
            pltpu.VMEM((total, hidden), kind),
            pltpu.VMEM((total, hidden), kind),
            pltpu.VMEM((dp_count, count, cap, cols), kind),
            pltpu.VMEM((count, cap, half), kind),
            pltpu.VMEM((count, cap, cols - half), kind),
            pltpu.VMEM((count, cap, cols), kind),
            pltpu.VMEM((count, cap, cols), kind),
            pltpu.VMEM((count, cap, cols), kind),
            pair,
            pair,
            dma((2, 2, count)),
            dma((2, 2, count)),
            pair,
            pair,
            dma((2,)),
            dma((2,)),
            pair,
            pair,
            pair,
            pair,
            pair,
            pair,
            dma((count,)),
            dma((count,)),
        ],
        compiler_params=pltpu.CompilerParams(
            collective_id=2, has_side_effects=True, vmem_limit_bytes=VMEM_LIMIT
        ),
        name="fused",
    )(sent_in, sent_dy, gate_t, up_t, down_w)
    return results[2:]


def body(tokens, out_grad, routes, gate_probs, w_gate, w_up, w_down):
    expert_count = lax.axis_size("expert")
    dp_count = lax.axis_size("dp")
    tok_count, width = tokens.shape
    top_count = routes.shape[1]
    capacity = 3 * tok_count * top_count // (2 * expert_count)
    capacity = -(-capacity // 8) * 8
    slot_total = expert_count * capacity
    flat_routes = routes.reshape(-1)
    order = jnp.arange(flat_routes.shape[0], dtype=jnp.int32)
    same = (flat_routes[:, None] == flat_routes[None, :]) & (order[None, :] < order[:, None])
    slot_index = jnp.sum(same.astype(jnp.int32), axis=1)
    destination = flat_routes * capacity + slot_index
    placing = jnp.arange(slot_total, dtype=jnp.int32)[:, None] == destination[None, :]
    weights = gate_probs.reshape(-1).astype(jnp.float32)
    by_token = placing.astype(jnp.bfloat16).reshape(slot_total, tok_count, top_count)
    collect = jnp.sum(by_token, axis=2)
    weighted = jnp.where(placing, weights[None, :], 0.0).astype(jnp.bfloat16)
    collect_weighted = jnp.sum(weighted.reshape(slot_total, tok_count, top_count), axis=2)
    sent_shape = (expert_count, capacity, width)
    sent_in = (
        jnp.dot(collect, tokens, preferred_element_type=jnp.float32)
        .astype(jnp.bfloat16)
        .reshape(sent_shape)
    )
    sent_dy = (
        jnp.dot(collect_weighted, out_grad, preferred_element_type=jnp.float32)
        .astype(jnp.bfloat16)
        .reshape(sent_shape)
    )
    contract_first = (((0,), (0,)), ((), ()))
    row_total = dp_count * slot_total
    if row_total <= 1024 and (dp_count * capacity) % 16 == 0:
        back, grad_gate, grad_up, grad_down = fused(
            sent_in, sent_dy, w_gate[0].T, w_up[0].T, w_down[0], dp_count
        )
        grad_gate, grad_up = grad_gate.T, grad_up.T
    else:
        all_in, all_dy = spread(sent_in, sent_dy, dp_count)
        rows_in = all_in.reshape(row_total, width)
        scaled = all_dy.reshape(row_total, width)
        gate_w = w_gate[0]
        up_w = w_up[0]
        down_w = w_down[0]
        contract_last = (((1,), (1,)), ((), ()))
        gate_pre = jnp.dot(rows_in, gate_w, preferred_element_type=jnp.float32)
        up_pre = jnp.dot(rows_in, up_w, preferred_element_type=jnp.float32)
        sigmoid_gate = jax.nn.sigmoid(gate_pre)
        active = gate_pre * sigmoid_gate
        hidden = (active * up_pre).astype(jnp.bfloat16)
        back_hidden = lax.dot_general(scaled, down_w, contract_last, preferred_element_type=jnp.float32)
        grad_gate_pre = (
            back_hidden * up_pre * sigmoid_gate * (1.0 + gate_pre * (1.0 - sigmoid_gate))
        ).astype(jnp.bfloat16)
        grad_up_pre = (back_hidden * active).astype(jnp.bfloat16)
        score = jnp.sum(back_hidden * hidden.astype(jnp.float32), axis=1, keepdims=True)
        score = jnp.broadcast_to(score, (row_total, LANES)).astype(jnp.bfloat16)
        back = gather(grad_gate_pre, grad_up_pre, score, gate_w, up_w, expert_count, dp_count)
        grad_down = lax.dot_general(
            hidden, scaled, contract_first, preferred_element_type=jnp.float32
        ).astype(jnp.bfloat16)
        grad_gate = lax.dot_general(
            rows_in, grad_gate_pre, contract_first, preferred_element_type=jnp.float32
        ).astype(jnp.bfloat16)
        grad_up = lax.dot_general(
            rows_in, grad_up_pre, contract_first, preferred_element_type=jnp.float32
        ).astype(jnp.bfloat16)
    back = back.reshape(slot_total, width + LANES)
    grad_tokens = lax.dot_general(
        collect, back[:, :width], contract_first, preferred_element_type=jnp.float32
    ).astype(jnp.bfloat16)
    picked = lax.dot_general(
        placing.astype(jnp.bfloat16),
        back[:, width:],
        contract_first,
        preferred_element_type=jnp.float32,
    )[:, 0]
    grad_probs = (picked / weights).astype(jnp.bfloat16).reshape(tok_count, top_count)
    return (grad_tokens, grad_probs, grad_gate[None], grad_up[None], grad_down[None])


def solution(mesh):
    in_specs = (
        P(("dp", "expert"), None),
        P(("dp", "expert"), None),
        P(("dp", "expert"), None),
        P(("dp", "expert"), None),
        P("expert", None, "dp"),
        P("expert", None, "dp"),
        P("expert", "dp", None),
    )
    out_specs = (
        P(("dp", "expert"), None),
        P(("dp", "expert"), None),
        P("expert", None, "dp"),
        P("expert", None, "dp"),
        P("expert", "dp", None),
    )
    return jax.shard_map(body, mesh=mesh, in_specs=in_specs, out_specs=out_specs, check_vma=False)
```

```python
import functools

import jax
import jax.numpy as jnp
from jax import lax
from jax.experimental import pallas as pl
from jax.experimental.pallas import tpu as pltpu
from jax.sharding import PartitionSpec as P

MESH = pl.DeviceIdType.MESH
LANES = 128
VMEM_LIMIT = 60 * 1024 * 1024


def partner(own, step, count):
    if count & (count - 1):
        return lax.rem(step - own + count, count)
    peer, bit = 0, 1
    while bit < count:
        mine, other = (own // bit) % 2, (step // bit) % 2
        peer = peer + bit * (mine + other - 2 * mine * other)
        bit *= 2
    return peer


def ring_places():
    own = lax.axis_index("dp")
    right = (2 * own + 1) % 5
    return own, right, 3 - right


def greet(count, own_e, right, left):
    barrier = pltpu.get_barrier_semaphore()
    for peer in (right, left):
        pl.semaphore_signal(barrier, inc=1, device_id={"dp": peer}, device_id_type=MESH)

    def step(k, carry):
        pl.semaphore_signal(
            barrier,
            inc=1,
            device_id={"expert": lax.rem(own_e + k, count)},
            device_id_type=MESH,
        )
        return carry

    lax.fori_loop(1, count, step, 0)
    pl.semaphore_wait(barrier, count + 1)


def remote(src, dst, send, recv, axis, peer):
    return pltpu.make_async_remote_copy(
        src_ref=src,
        dst_ref=dst,
        send_sem=send,
        recv_sem=recv,
        device_id={axis: peer},
        device_id_type=MESH,
    )


def spread_kernel(count, sent_in, sent_dy, all_in, all_dy, z_s, z_r, side_s, side_r, far_s, far_r, own_sem):
    own_e = lax.axis_index("expert")
    own_d, right, left = ring_places()
    sent, full = (sent_in, sent_dy), (all_in, all_dy)
    sides = (right, left)

    def z_copy(a, i):
        peer = partner(own_e, i, count)
        return remote(
            sent[a].at[peer], full[a].at[own_d, own_e], z_s.at[a, i], z_r.at[a, i], "expert", peer
        )

    def z_landed(a, i):
        place = full[a].at[own_d, partner(own_e, i, count)]
        return remote(place, place, z_s.at[a, i], z_r.at[a, i], "expert", own_e)

    def side_copy(a, way, i, src=None):
        place = full[a].at[own_d, partner(own_e, i, count)]
        return remote(
            place if src is None else src, place, side_s.at[a, way, i], side_r.at[a, way, i], "dp", sides[way]
        )

    def side_landed(a, way, i):
        place = full[a].at[sides[1 - way], partner(own_e, i, count)]
        return remote(place, place, side_s.at[a, way, i], side_r.at[a, way, i], "dp", sides[way])

    def far_copy(a, i):
        place = full[a].at[sides[1 - a], partner(own_e, i, count)]
        return remote(place, place, far_s.at[a, i], far_r.at[a, i], "dp", sides[a])

    def far_landed(a, i):
        place = full[a].at[3 - own_d, partner(own_e, i, count)]
        return remote(place, place, far_s.at[a, i], far_r.at[a, i], "dp", sides[a])

    own = [
        pltpu.make_async_copy(sent[a].at[own_e], full[a].at[own_d, own_e], own_sem.at[a])
        for a in range(2)
    ]
    for a in range(2):
        own[a].start()
    greet(count, own_e, right, left)
    for a in range(2):
        for way in range(2):
            side_copy(a, way, 0, sent[a].at[own_e]).start()

    def start(i, carry):
        for a in range(2):
            z_copy(a, i).start()
        return carry

    lax.fori_loop(1, count, start, 0)

    def onward(i):
        for a in range(2):
            side_landed(a, a, i).wait_recv()
            far_copy(a, i).start()

    def relay(i, carry):
        for a in range(2):
            z_landed(a, i).wait_recv()
            for way in range(2):
                side_copy(a, way, i).start()
        onward(i - 1)
        return carry

    lax.fori_loop(1, count, relay, 0)
    onward(count - 1)

    def finish(i, carry):
        for a in range(2):
            side_landed(a, 1 - a, i).wait_recv()
            far_landed(a, i).wait_recv()
            far_copy(a, i).wait_send()
            for way in range(2):
                side_copy(a, way, i).wait_send()
        return carry

    lax.fori_loop(0, count, finish, 0)

    def sent_off(i, carry):
        for a in range(2):
            z_copy(a, i).wait_send()
        return carry

    lax.fori_loop(1, count, sent_off, 0)
    for a in range(2):
        own[a].wait()


def spread(sent_in, sent_dy, dp_count):
    count = sent_in.shape[0]
    shape = jax.ShapeDtypeStruct((dp_count,) + sent_in.shape, sent_in.dtype)
    dma = pltpu.SemaphoreType.DMA
    return pl.pallas_call(
        functools.partial(spread_kernel, count),
        out_shape=(shape, shape),
        in_specs=[pl.BlockSpec(memory_space=pl.ANY)] * 2,
        out_specs=[pl.BlockSpec(memory_space=pl.ANY)] * 2,
        scratch_shapes=[
            dma((2, count)),
            dma((2, count)),
            dma((2, 2, count)),
            dma((2, 2, count)),
            dma((2, count)),
            dma((2, count)),
            dma((2,)),
        ],
        compiler_params=pltpu.CompilerParams(
            collective_id=0, has_side_effects=True, vmem_limit_bytes=VMEM_LIMIT
        ),
        name="spread",
    )(sent_in, sent_dy)


def col_tiles(first, last, width):
    while first < last:
        yield slice(first, min(first + width, last))
        first = min(first + width, last)


def gather_kernel(
    count, chunks, gg, gu, score, gate_w, up_w, back, part, far_l, far_r, near_l, near_r, zed,
    far_s, far_rs, side_s, side_rs, sum_s, sum_rs, z_s, z_r, own_sem,
):
    own_e = lax.axis_index("expert")
    own_d, right, left = ring_places()
    width = gate_w.shape[0]
    rows = part.shape[1]
    cols = part.shape[2]
    cap = rows // count
    step_rows = rows // chunks
    slabs = count // chunks
    half = width // 2
    halves = (pl.ds(0, half), pl.ds(half, cols - half))
    spans = ((0, half), (half, cols))
    sides = (right, left)
    far_in = (far_l, far_r)
    near_in = (near_l, near_r)
    targets = (right, left, 3 - own_d, own_d)
    tile = 512

    def rows_at(c):
        return pl.ds(pl.multiple_of(c * step_rows, step_rows), step_rows)

    def far_copy(way, c):
        return remote(
            part.at[2, rows_at(c), halves[way]], far_in[way].at[rows_at(c)],
            far_s.at[way, c], far_rs.at[way, c], "dp", sides[way],
        )

    def side_copy(way, c):
        return remote(
            part.at[way, rows_at(c), halves[1 - way]], near_in[way].at[rows_at(c), halves[1 - way]],
            side_s.at[way, c], side_rs.at[way, c], "dp", sides[way],
        )

    def sum_copy(way, c):
        return remote(
            part.at[way, rows_at(c), halves[way]], near_in[way].at[rows_at(c), halves[way]],
            sum_s.at[way, c], sum_rs.at[way, c], "dp", sides[way],
        )

    def compute(slot):
        row0 = pl.multiple_of(targets[slot] * rows, rows)
        g = gg[pl.ds(row0, rows), :]
        u = gu[pl.ds(row0, rows), :]
        part[slot, :, width:cols] = score[pl.ds(row0, rows), :]

        def one(j, carry):
            at = pl.ds(pl.multiple_of(j * tile, tile), tile)
            dims = (((1,), (1,)), ((), ()))
            value = lax.dot_general(g, gate_w[at, :], dims, preferred_element_type=jnp.float32)
            value = value + lax.dot_general(u, up_w[at, :], dims, preferred_element_type=jnp.float32)
            part[slot, :, at] = value.astype(part.dtype)
            return carry

        lax.fori_loop(0, width // tile, one, 0)

    def for_chunks(f):
        def go(c, carry):
            f(c)
            return carry

        lax.fori_loop(0, chunks, go, 0)

    greet(count, own_e, right, left)
    compute(2)

    @for_chunks
    def _(c):
        for way in range(2):
            far_copy(way, c).start()

    for way in range(2):
        compute(way)

        @for_chunks
        def _(c):
            side_copy(way, c).start()

    compute(3)

    @for_chunks
    def _(c):
        for way in range(2):
            far_copy(way, c).wait_recv()
            for at in col_tiles(*spans[way], tile):
                there = slice(at.start - spans[way][0], at.stop - spans[way][0])
                total = part[way, rows_at(c), at].astype(jnp.float32) + far_in[way][
                    rows_at(c), there
                ].astype(jnp.float32)
                part[way, rows_at(c), at] = total.astype(part.dtype)
            sum_copy(way, c).start()

    def z_copy(i):
        peer = partner(own_e, i, count)
        return remote(zed.at[peer], back.at[own_e], z_s.at[i], z_r.at[i], "expert", peer)

    def z_landed(i):
        place = back.at[partner(own_e, i, count)]
        return remote(place, place, z_s.at[i], z_r.at[i], "expert", own_e)

    def merge(c):
        for way in range(2):
            side_copy(way, c).wait_recv()
            sum_copy(way, c).wait_recv()
        for at in col_tiles(0, cols, tile):
            total = part[3, rows_at(c), at].astype(jnp.float32)
            total = total + near_l[rows_at(c), at].astype(jnp.float32)
            total = total + near_r[rows_at(c), at].astype(jnp.float32)
            total = total.reshape(slabs, cap, at.stop - at.start)
            zed[pl.ds(c * slabs, slabs), :, at] = total.astype(zed.dtype)

    @for_chunks
    def _(c):
        merge(c)
        for k in range(slabs):
            there = c * slabs + k
            step = partner(own_e, there, count)

            @pl.when(there != own_e)
            def _():
                z_copy(step).start()

    own = pltpu.make_async_copy(zed.at[own_e], back.at[own_e], own_sem.at[0])
    own.start()
    own.wait()

    def landed(i, carry):
        z_landed(i).wait_recv()
        z_copy(i).wait_send()
        return carry

    lax.fori_loop(1, count, landed, 0)

    @for_chunks
    def _(c):
        for way in range(2):
            far_copy(way, c).wait_send()
            side_copy(way, c).wait_send()
            sum_copy(way, c).wait_send()


def gather(gg, gu, score, gate_w, up_w, count, dp_count):
    width = gate_w.shape[0]
    rows = gg.shape[0] // dp_count
    cols = width + LANES
    half = width // 2
    chunks = 4 if count % 4 == 0 and (rows // 4) % 16 == 0 else 1
    dma = pltpu.SemaphoreType.DMA
    kind = jnp.bfloat16
    pairs = dma((2, chunks))
    return pl.pallas_call(
        functools.partial(gather_kernel, count, chunks),
        out_shape=jax.ShapeDtypeStruct((count, rows // count, cols), kind),
        in_specs=[pl.BlockSpec(memory_space=pltpu.VMEM)] * 5,
        out_specs=pl.BlockSpec(memory_space=pl.ANY),
        scratch_shapes=[
            pltpu.VMEM((4, rows, cols), kind),
            pltpu.VMEM((rows, half), kind),
            pltpu.VMEM((rows, cols - half), kind),
            pltpu.VMEM((rows, cols), kind),
            pltpu.VMEM((rows, cols), kind),
            pltpu.VMEM((count, rows // count, cols), kind),
            pairs,
            pairs,
            pairs,
            pairs,
            pairs,
            pairs,
            dma((count,)),
            dma((count,)),
            dma((1,)),
        ],
        compiler_params=pltpu.CompilerParams(
            collective_id=1, has_side_effects=True, vmem_limit_bytes=VMEM_LIMIT
        ),
        name="gather",
    )(gg, gu, score, gate_w, up_w)


def fused_kernel(
    count, sent_in, sent_dy, gate_w, up_w, down_w,
    all_in, all_dy, back, grad_gate, grad_up, grad_down,
    stage, flat_in, flat_dy, hid, dgate, dup, part, far_l, far_r, near_l, near_r, zed, total,
    z_s, z_r, side_s, side_r, far_s, far_r_sem, own_sem, stage_sem,
    rf_s, rf_r, rd_s, rd_r, rs_s, rs_r, home_s, home_r,
):
    own_e = lax.axis_index("expert")
    own_d, right, left = ring_places()
    sent, full, flat = (sent_in, sent_dy), (all_in, all_dy), (flat_in, flat_dy)
    sides = (right, left)
    dp_count, _, cap, width = all_in.shape
    cols = part.shape[3]
    group = dp_count * cap
    half = width // 2
    halves = (pl.ds(0, half), pl.ds(half, cols - half))
    spans = ((0, half), (half, cols))
    far_in, near_in = (far_l, far_r), (near_l, near_r)
    tile = 512
    last_dims = (((1,), (1,)), ((), ()))
    first_dims = (((0,), (0,)), ((), ()))

    def z_copy(a, i):
        peer = partner(own_e, i, count)
        return remote(
            sent[a].at[peer], full[a].at[own_d, own_e], z_s.at[a, i], z_r.at[a, i], "expert", peer
        )

    def z_landed(a, i):
        place = full[a].at[own_d, partner(own_e, i, count)]
        return remote(place, place, z_s.at[a, i], z_r.at[a, i], "expert", own_e)

    def side_copy(a, way, i, src=None):
        place = full[a].at[own_d, partner(own_e, i, count)]
        return remote(
            place if src is None else src, place, side_s.at[a, way, i], side_r.at[a, way, i], "dp", sides[way]
        )

    def side_landed(a, way, i):
        place = full[a].at[sides[1 - way], partner(own_e, i, count)]
        return remote(place, place, side_s.at[a, way, i], side_r.at[a, way, i], "dp", sides[way])

    def onward_copy(a, i):
        place = full[a].at[sides[1 - a], partner(own_e, i, count)]
        return remote(place, place, far_s.at[a, i], far_r_sem.at[a, i], "dp", sides[a])

    def onward_landed(a, i):
        place = full[a].at[3 - own_d, partner(own_e, i, count)]
        return remote(place, place, far_s.at[a, i], far_r_sem.at[a, i], "dp", sides[a])

    def rf_copy(way, c):
        return remote(
            part.at[3 - own_d, c, :, halves[way]], far_in[way].at[c],
            rf_s.at[way, c], rf_r.at[way, c], "dp", sides[way],
        )

    def rd_copy(way, c):
        return remote(
            part.at[sides[way], c, :, halves[1 - way]], near_in[way].at[c, :, halves[1 - way]],
            rd_s.at[way, c], rd_r.at[way, c], "dp", sides[way],
        )

    def rs_copy(way, c):
        return remote(
            part.at[sides[way], c, :, halves[way]], near_in[way].at[c, :, halves[way]],
            rs_s.at[way, c], rs_r.at[way, c], "dp", sides[way],
        )

    def home_copy(i):
        peer = partner(own_e, i, count)
        return remote(zed.at[i], back.at[own_e], home_s.at[i], home_r.at[i], "expert", peer)

    def home_landed(i):
        place = back.at[partner(own_e, i, count)]
        return remote(place, place, home_s.at[i], home_r.at[i], "expert", own_e)

    own = [
        pltpu.make_async_copy(sent[a].at[own_e], full[a].at[own_d, own_e], own_sem.at[a])
        for a in range(2)
    ]
    for a in range(2):
        own[a].start()
    greet(count, own_e, right, left)
    for a in range(2):
        for way in range(2):
            side_copy(a, way, 0, sent[a].at[own_e]).start()

    def start(i, carry):
        for a in range(2):
            z_copy(a, i).start()
        return carry

    lax.fori_loop(1, count, start, 0)
    for a in range(2):
        own[a].wait()

    def relay(i):
        for a in range(2):
            z_landed(a, i).wait_recv()
            for way in range(2):
                side_copy(a, way, i).start()

    def onward(i):
        for a in range(2):
            side_landed(a, a, i).wait_recv()
            onward_copy(a, i).start()

    def compute(i):
        src = partner(own_e, i, count)
        for a in range(2):
            side_landed(a, 1 - a, i).wait_recv()
            onward_landed(a, i).wait_recv()
        loads = [
            pltpu.make_async_copy(full[a].at[:, src], stage.at[a], stage_sem.at[a])
            for a in range(2)
        ]
        for load in loads:
            load.start()
        for load in loads:
            load.wait()
        rows = pl.ds(pl.multiple_of(i * group, group), group)
        for a in range(2):
            for at in col_tiles(0, width, tile):
                value = stage[a, :, :, at].astype(jnp.float32).reshape(group, tile)
                flat[a][rows, at] = value.astype(flat[a].dtype)

        def product(x, w):
            return lax.dot_general(x, w, last_dims, preferred_element_type=jnp.float32)

        gate_pre = product(flat_in[rows, :], gate_w[...])
        up_pre = product(flat_in[rows, :], up_w[...])
        back_hidden = product(flat_dy[rows, :], down_w[...])
        sigmoid_gate = jax.nn.sigmoid(gate_pre)
        active = gate_pre * sigmoid_gate
        hidden = (active * up_pre).astype(jnp.bfloat16)
        score = jnp.sum(back_hidden * hidden.astype(jnp.float32), axis=1, keepdims=True)
        g = (back_hidden * up_pre * sigmoid_gate * (1.0 + gate_pre * (1.0 - sigmoid_gate))).astype(
            jnp.bfloat16
        )
        u = (back_hidden * active).astype(jnp.bfloat16)
        hid[rows, :] = hidden
        dgate[rows, :] = g
        dup[rows, :] = u
        score = jnp.broadcast_to(score, (group, cols - width)).reshape(dp_count, cap, cols - width)
        part[:, i, :, width:cols] = score.astype(part.dtype)
        for at in col_tiles(0, width, tile):
            value = jnp.dot(g, gate_w[:, at], preferred_element_type=jnp.float32)
            value = value + jnp.dot(u, up_w[:, at], preferred_element_type=jnp.float32)
            part[:, i, :, at] = value.reshape(dp_count, cap, tile).astype(part.dtype)
        for way in range(2):
            rf_copy(way, i).start()
        for way in range(2):
            rd_copy(way, i).start()

    def ring_sum(i):
        for way in range(2):
            rf_copy(way, i).wait_recv()
            for at in col_tiles(*spans[way], tile):
                there = slice(at.start - spans[way][0], at.stop - spans[way][0])
                summed = part[sides[way], i, :, at].astype(jnp.float32)
                summed = summed + far_in[way][i, :, there].astype(jnp.float32)
                part[sides[way], i, :, at] = summed.astype(part.dtype)
            rs_copy(way, i).start()

    def merge(i):
        for way in range(2):
            rd_copy(way, i).wait_recv()
            rs_copy(way, i).wait_recv()
        for at in col_tiles(0, cols, tile):
            summed = part[own_d, i, :, at].astype(jnp.float32)
            summed = summed + near_l[i, :, at].astype(jnp.float32)
            summed = summed + near_r[i, :, at].astype(jnp.float32)
            zed[i, :, at] = summed.astype(zed.dtype)

        @pl.when(i > 0)
        def _():
            home_copy(i).start()

    def weight_grad(k, out, left_rows, right_rows, pair):
        rows = pl.ds(pl.multiple_of(pair * 2 * group, 2 * group), 2 * group)
        left_part = left_rows[rows, :]

        def one(j, carry):
            at = pl.ds(pl.multiple_of(j * tile, tile), tile)
            value = lax.dot_general(
                left_part, right_rows[rows, at], first_dims, preferred_element_type=jnp.float32
            )

            @pl.when(pair == 0)
            def _():
                total[k, :, at] = value

            @pl.when((pair > 0) & (pair < count // 2 - 1))
            def _():
                total[k, :, at] += value

            @pl.when(pair == count // 2 - 1)
            def _():
                out[:, at] = (total[k, :, at] + value).astype(out.dtype)

            return carry

        lax.fori_loop(0, width // tile, one, 0)

    grads = ((grad_down, hid, flat_dy), (grad_gate, dgate, flat_in), (grad_up, dup, flat_in))

    def step(t, carry):
        def during(lag, first, f):
            @pl.when((t - lag >= first) & (t - lag < count))
            def _():
                f(t - lag)

        during(0, 1, relay)
        during(1, 0, onward)
        during(3, 0, ring_sum)
        during(2, 0, compute)
        during(4, 0, merge)

        @pl.when((t >= 4) & (t < count + 4) & (t % 2 == 0))
        def _():
            for k, grad in enumerate(grads):
                weight_grad(k, *grad, (t - 4) // 2)

        return carry

    lax.fori_loop(0, count + 4, step, 0)
    keep = pltpu.make_async_copy(zed.at[0], back.at[own_e], own_sem.at[0])
    keep.start()
    keep.wait()

    def finish(i, carry):
        for a in range(2):
            onward_copy(a, i).wait_send()
            for way in range(2):
                side_copy(a, way, i).wait_send()
        for way in range(2):
            rf_copy(way, i).wait_send()
            rd_copy(way, i).wait_send()
            rs_copy(way, i).wait_send()
        return carry

    lax.fori_loop(0, count, finish, 0)

    def landed(i, carry):
        for a in range(2):
            z_copy(a, i).wait_send()
        home_landed(i).wait_recv()
        home_copy(i).wait_send()
        return carry

    lax.fori_loop(1, count, landed, 0)


def fused(sent_in, sent_dy, gate_t, up_t, down_w, dp_count):
    count, cap, width = sent_in.shape
    kind = sent_in.dtype
    hidden = down_w.shape[0]
    cols, half = width + LANES, width // 2
    row_count = dp_count * count * cap
    dma = pltpu.SemaphoreType.DMA
    full = jax.ShapeDtypeStruct((dp_count, count, cap, width), kind)
    grad = jax.ShapeDtypeStruct((hidden, width), kind)
    whole = pl.BlockSpec(memory_space=pltpu.VMEM)
    apart = pl.BlockSpec(memory_space=pl.ANY)
    pair = dma((2, count))
    results = pl.pallas_call(
        functools.partial(fused_kernel, count),
        out_shape=(full, full, jax.ShapeDtypeStruct((count, cap, cols), kind), grad, grad, grad),
        in_specs=[apart, apart, whole, whole, whole],
        out_specs=[apart, apart, apart, whole, whole, whole],
        scratch_shapes=[
            pltpu.VMEM((2, dp_count, cap, width), kind),
            pltpu.VMEM((row_count, width), kind),
            pltpu.VMEM((row_count, width), kind),
            pltpu.VMEM((row_count, hidden), kind),
            pltpu.VMEM((row_count, hidden), kind),
            pltpu.VMEM((row_count, hidden), kind),
            pltpu.VMEM((dp_count, count, cap, cols), kind),
            pltpu.VMEM((count, cap, half), kind),
            pltpu.VMEM((count, cap, cols - half), kind),
            pltpu.VMEM((count, cap, cols), kind),
            pltpu.VMEM((count, cap, cols), kind),
            pltpu.VMEM((count, cap, cols), kind),
            pltpu.VMEM((3, hidden, width), jnp.float32),
            pair,
            pair,
            dma((2, 2, count)),
            dma((2, 2, count)),
            pair,
            pair,
            dma((2,)),
            dma((2,)),
            pair,
            pair,
            pair,
            pair,
            pair,
            pair,
            dma((count,)),
            dma((count,)),
        ],
        compiler_params=pltpu.CompilerParams(
            collective_id=2, has_side_effects=True, vmem_limit_bytes=VMEM_LIMIT
        ),
        name="fused",
    )(sent_in, sent_dy, gate_t, up_t, down_w)
    return results[2:]


def body(tokens, out_grad, routes, gate_probs, w_gate, w_up, w_down):
    expert_count = lax.axis_size("expert")
    dp_count = lax.axis_size("dp")
    tok_count, width = tokens.shape
    top_count = routes.shape[1]
    capacity = 3 * tok_count * top_count // (2 * expert_count)
    capacity = -(-capacity // 8) * 8
    slot_total = expert_count * capacity
    flat_routes = routes.reshape(-1)
    order = jnp.arange(flat_routes.shape[0], dtype=jnp.int32)
    same = (flat_routes[:, None] == flat_routes[None, :]) & (order[None, :] < order[:, None])
    slot_index = jnp.sum(same.astype(jnp.int32), axis=1)
    destination = flat_routes * capacity + slot_index
    placing = jnp.arange(slot_total, dtype=jnp.int32)[:, None] == destination[None, :]
    weights = gate_probs.reshape(-1).astype(jnp.float32)
    by_token = placing.astype(jnp.bfloat16).reshape(slot_total, tok_count, top_count)
    collect = jnp.sum(by_token, axis=2)
    weighted = jnp.where(placing, weights[None, :], 0.0).astype(jnp.bfloat16)
    collect_weighted = jnp.sum(weighted.reshape(slot_total, tok_count, top_count), axis=2)
    sent_shape = (expert_count, capacity, width)
    sent_in = (
        jnp.dot(collect, tokens, preferred_element_type=jnp.float32)
        .astype(jnp.bfloat16)
        .reshape(sent_shape)
    )
    sent_dy = (
        jnp.dot(collect_weighted, out_grad, preferred_element_type=jnp.float32)
        .astype(jnp.bfloat16)
        .reshape(sent_shape)
    )
    contract_first = (((0,), (0,)), ((), ()))
    row_total = dp_count * slot_total
    if row_total <= 1024 and expert_count % 2 == 0 and (dp_count * capacity) % 16 == 0:
        back, grad_gate, grad_up, grad_down = fused(
            sent_in, sent_dy, w_gate[0].T, w_up[0].T, w_down[0], dp_count
        )
        grad_gate, grad_up = grad_gate.T, grad_up.T
    else:
        all_in, all_dy = spread(sent_in, sent_dy, dp_count)
        rows_in = all_in.reshape(row_total, width)
        scaled = all_dy.reshape(row_total, width)
        gate_w = w_gate[0]
        up_w = w_up[0]
        down_w = w_down[0]
        contract_last = (((1,), (1,)), ((), ()))
        gate_pre = jnp.dot(rows_in, gate_w, preferred_element_type=jnp.float32)
        up_pre = jnp.dot(rows_in, up_w, preferred_element_type=jnp.float32)
        sigmoid_gate = jax.nn.sigmoid(gate_pre)
        active = gate_pre * sigmoid_gate
        hidden = (active * up_pre).astype(jnp.bfloat16)
        back_hidden = lax.dot_general(scaled, down_w, contract_last, preferred_element_type=jnp.float32)
        grad_gate_pre = (
            back_hidden * up_pre * sigmoid_gate * (1.0 + gate_pre * (1.0 - sigmoid_gate))
        ).astype(jnp.bfloat16)
        grad_up_pre = (back_hidden * active).astype(jnp.bfloat16)
        score = jnp.sum(back_hidden * hidden.astype(jnp.float32), axis=1, keepdims=True)
        score = jnp.broadcast_to(score, (row_total, LANES)).astype(jnp.bfloat16)
        back = gather(grad_gate_pre, grad_up_pre, score, gate_w, up_w, expert_count, dp_count)
        grad_down = lax.dot_general(
            hidden, scaled, contract_first, preferred_element_type=jnp.float32
        ).astype(jnp.bfloat16)
        grad_gate = lax.dot_general(
            rows_in, grad_gate_pre, contract_first, preferred_element_type=jnp.float32
        ).astype(jnp.bfloat16)
        grad_up = lax.dot_general(
            rows_in, grad_up_pre, contract_first, preferred_element_type=jnp.float32
        ).astype(jnp.bfloat16)
    back = back.reshape(slot_total, width + LANES)
    grad_tokens = lax.dot_general(
        collect, back[:, :width], contract_first, preferred_element_type=jnp.float32
    ).astype(jnp.bfloat16)
    picked = lax.dot_general(
        placing.astype(jnp.bfloat16),
        back[:, width:],
        contract_first,
        preferred_element_type=jnp.float32,
    )[:, 0]
    grad_probs = (picked / weights).astype(jnp.bfloat16).reshape(tok_count, top_count)
    return (grad_tokens, grad_probs, grad_gate[None], grad_up[None], grad_down[None])


def solution(mesh):
    in_specs = (
        P(("dp", "expert"), None),
        P(("dp", "expert"), None),
        P(("dp", "expert"), None),
        P(("dp", "expert"), None),
        P("expert", None, "dp"),
        P("expert", None, "dp"),
        P("expert", "dp", None),
    )
    out_specs = (
        P(("dp", "expert"), None),
        P(("dp", "expert"), None),
        P("expert", None, "dp"),
        P("expert", None, "dp"),
        P("expert", "dp", None),
    )
    return jax.shard_map(body, mesh=mesh, in_specs=in_specs, out_specs=out_specs, check_vma=False)
```

```python
import functools

import jax
import jax.numpy as jnp
from jax import lax
from jax.experimental import pallas as pl
from jax.experimental.pallas import tpu as pltpu
from jax.sharding import PartitionSpec as P

MESH = pl.DeviceIdType.MESH
LANES = 128
VMEM_LIMIT = 60 * 1024 * 1024


def partner(own, step, count):
    if count & (count - 1):
        return lax.rem(step - own + count, count)
    peer, bit = 0, 1
    while bit < count:
        mine, other = (own // bit) % 2, (step // bit) % 2
        peer = peer + bit * (mine + other - 2 * mine * other)
        bit *= 2
    return peer


def ring_places():
    own = lax.axis_index("dp")
    right = (2 * own + 1) % 5
    return own, right, 3 - right


def greet(count, own_e, right, left):
    barrier = pltpu.get_barrier_semaphore()
    for peer in (right, left):
        pl.semaphore_signal(barrier, inc=1, device_id={"dp": peer}, device_id_type=MESH)

    def step(k, carry):
        pl.semaphore_signal(
            barrier,
            inc=1,
            device_id={"expert": lax.rem(own_e + k, count)},
            device_id_type=MESH,
        )
        return carry

    lax.fori_loop(1, count, step, 0)
    pl.semaphore_wait(barrier, count + 1)


def remote(src, dst, send, recv, axis, peer):
    return pltpu.make_async_remote_copy(
        src_ref=src,
        dst_ref=dst,
        send_sem=send,
        recv_sem=recv,
        device_id={axis: peer},
        device_id_type=MESH,
    )


def spread_kernel(count, sent_in, sent_dy, all_in, all_dy, z_s, z_r, side_s, side_r, far_s, far_r, own_sem):
    own_e = lax.axis_index("expert")
    own_d, right, left = ring_places()
    sent, full = (sent_in, sent_dy), (all_in, all_dy)
    sides = (right, left)

    def z_copy(a, i):
        peer = partner(own_e, i, count)
        return remote(
            sent[a].at[peer], full[a].at[own_d, own_e], z_s.at[a, i], z_r.at[a, i], "expert", peer
        )

    def z_landed(a, i):
        place = full[a].at[own_d, partner(own_e, i, count)]
        return remote(place, place, z_s.at[a, i], z_r.at[a, i], "expert", own_e)

    def side_copy(a, way, i, src=None):
        place = full[a].at[own_d, partner(own_e, i, count)]
        return remote(
            place if src is None else src, place, side_s.at[a, way, i], side_r.at[a, way, i], "dp", sides[way]
        )

    def side_landed(a, way, i):
        place = full[a].at[sides[1 - way], partner(own_e, i, count)]
        return remote(place, place, side_s.at[a, way, i], side_r.at[a, way, i], "dp", sides[way])

    def far_copy(a, i):
        place = full[a].at[sides[1 - a], partner(own_e, i, count)]
        return remote(place, place, far_s.at[a, i], far_r.at[a, i], "dp", sides[a])

    def far_landed(a, i):
        place = full[a].at[3 - own_d, partner(own_e, i, count)]
        return remote(place, place, far_s.at[a, i], far_r.at[a, i], "dp", sides[a])

    own = [
        pltpu.make_async_copy(sent[a].at[own_e], full[a].at[own_d, own_e], own_sem.at[a])
        for a in range(2)
    ]
    for a in range(2):
        own[a].start()
    greet(count, own_e, right, left)
    for a in range(2):
        for way in range(2):
            side_copy(a, way, 0, sent[a].at[own_e]).start()

    def start(i, carry):
        for a in range(2):
            z_copy(a, i).start()
        return carry

    lax.fori_loop(1, count, start, 0)

    def onward(i):
        for a in range(2):
            side_landed(a, a, i).wait_recv()
            far_copy(a, i).start()

    def relay(i, carry):
        for a in range(2):
            z_landed(a, i).wait_recv()
            for way in range(2):
                side_copy(a, way, i).start()
        onward(i - 1)
        return carry

    lax.fori_loop(1, count, relay, 0)
    onward(count - 1)

    def finish(i, carry):
        for a in range(2):
            side_landed(a, 1 - a, i).wait_recv()
            far_landed(a, i).wait_recv()
            far_copy(a, i).wait_send()
            for way in range(2):
                side_copy(a, way, i).wait_send()
        return carry

    lax.fori_loop(0, count, finish, 0)

    def sent_off(i, carry):
        for a in range(2):
            z_copy(a, i).wait_send()
        return carry

    lax.fori_loop(1, count, sent_off, 0)
    for a in range(2):
        own[a].wait()


def spread(sent_in, sent_dy, dp_count):
    count = sent_in.shape[0]
    shape = jax.ShapeDtypeStruct((dp_count,) + sent_in.shape, sent_in.dtype)
    dma = pltpu.SemaphoreType.DMA
    return pl.pallas_call(
        functools.partial(spread_kernel, count),
        out_shape=(shape, shape),
        in_specs=[pl.BlockSpec(memory_space=pl.ANY)] * 2,
        out_specs=[pl.BlockSpec(memory_space=pl.ANY)] * 2,
        scratch_shapes=[
            dma((2, count)),
            dma((2, count)),
            dma((2, 2, count)),
            dma((2, 2, count)),
            dma((2, count)),
            dma((2, count)),
            dma((2,)),
        ],
        compiler_params=pltpu.CompilerParams(
            collective_id=0, has_side_effects=True, vmem_limit_bytes=VMEM_LIMIT
        ),
        name="spread",
    )(sent_in, sent_dy)


def col_tiles(first, last, width):
    while first < last:
        yield slice(first, min(first + width, last))
        first = min(first + width, last)


def gather_kernel(
    count, chunks, gg, gu, score, gate_w, up_w, back, part, far_l, far_r, near_l, near_r, zed,
    far_s, far_rs, side_s, side_rs, sum_s, sum_rs, z_s, z_r, own_sem,
):
    own_e = lax.axis_index("expert")
    own_d, right, left = ring_places()
    width = gate_w.shape[0]
    rows = part.shape[1]
    cols = part.shape[2]
    cap = rows // count
    step_rows = rows // chunks
    slabs = count // chunks
    half = width // 2
    halves = (pl.ds(0, half), pl.ds(half, cols - half))
    spans = ((0, half), (half, cols))
    sides = (right, left)
    far_in = (far_l, far_r)
    near_in = (near_l, near_r)
    targets = (right, left, 3 - own_d, own_d)
    tile = 512

    def rows_at(c):
        return pl.ds(pl.multiple_of(c * step_rows, step_rows), step_rows)

    def far_copy(way, c):
        return remote(
            part.at[2, rows_at(c), halves[way]], far_in[way].at[rows_at(c)],
            far_s.at[way, c], far_rs.at[way, c], "dp", sides[way],
        )

    def side_copy(way, c):
        return remote(
            part.at[way, rows_at(c), halves[1 - way]], near_in[way].at[rows_at(c), halves[1 - way]],
            side_s.at[way, c], side_rs.at[way, c], "dp", sides[way],
        )

    def sum_copy(way, c):
        return remote(
            part.at[way, rows_at(c), halves[way]], near_in[way].at[rows_at(c), halves[way]],
            sum_s.at[way, c], sum_rs.at[way, c], "dp", sides[way],
        )

    def compute(slot):
        row0 = pl.multiple_of(targets[slot] * rows, rows)
        g = gg[pl.ds(row0, rows), :]
        u = gu[pl.ds(row0, rows), :]
        part[slot, :, width:cols] = score[pl.ds(row0, rows), :]

        def one(j, carry):
            at = pl.ds(pl.multiple_of(j * tile, tile), tile)
            dims = (((1,), (1,)), ((), ()))
            value = lax.dot_general(g, gate_w[at, :], dims, preferred_element_type=jnp.float32)
            value = value + lax.dot_general(u, up_w[at, :], dims, preferred_element_type=jnp.float32)
            part[slot, :, at] = value.astype(part.dtype)
            return carry

        lax.fori_loop(0, width // tile, one, 0)

    def for_chunks(f):
        def go(c, carry):
            f(c)
            return carry

        lax.fori_loop(0, chunks, go, 0)

    greet(count, own_e, right, left)
    compute(2)

    @for_chunks
    def _(c):
        for way in range(2):
            far_copy(way, c).start()

    for way in range(2):
        compute(way)

        @for_chunks
        def _(c):
            side_copy(way, c).start()

    compute(3)

    @for_chunks
    def _(c):
        for way in range(2):
            far_copy(way, c).wait_recv()
            for at in col_tiles(*spans[way], tile):
                there = slice(at.start - spans[way][0], at.stop - spans[way][0])
                total = part[way, rows_at(c), at].astype(jnp.float32) + far_in[way][
                    rows_at(c), there
                ].astype(jnp.float32)
                part[way, rows_at(c), at] = total.astype(part.dtype)
            sum_copy(way, c).start()

    def z_copy(i):
        peer = partner(own_e, i, count)
        return remote(zed.at[peer], back.at[own_e], z_s.at[i], z_r.at[i], "expert", peer)

    def z_landed(i):
        place = back.at[partner(own_e, i, count)]
        return remote(place, place, z_s.at[i], z_r.at[i], "expert", own_e)

    def merge(c):
        for way in range(2):
            side_copy(way, c).wait_recv()
            sum_copy(way, c).wait_recv()
        for at in col_tiles(0, cols, tile):
            total = part[3, rows_at(c), at].astype(jnp.float32)
            total = total + near_l[rows_at(c), at].astype(jnp.float32)
            total = total + near_r[rows_at(c), at].astype(jnp.float32)
            total = total.reshape(slabs, cap, at.stop - at.start)
            zed[pl.ds(c * slabs, slabs), :, at] = total.astype(zed.dtype)

    @for_chunks
    def _(c):
        merge(c)
        for k in range(slabs):
            there = c * slabs + k
            step = partner(own_e, there, count)

            @pl.when(there != own_e)
            def _():
                z_copy(step).start()

    own = pltpu.make_async_copy(zed.at[own_e], back.at[own_e], own_sem.at[0])
    own.start()
    own.wait()

    def landed(i, carry):
        z_landed(i).wait_recv()
        z_copy(i).wait_send()
        return carry

    lax.fori_loop(1, count, landed, 0)

    @for_chunks
    def _(c):
        for way in range(2):
            far_copy(way, c).wait_send()
            side_copy(way, c).wait_send()
            sum_copy(way, c).wait_send()


def gather(gg, gu, score, gate_w, up_w, count, dp_count):
    width = gate_w.shape[0]
    rows = gg.shape[0] // dp_count
    cols = width + LANES
    half = width // 2
    chunks = 4 if count % 4 == 0 and (rows // 4) % 16 == 0 else 1
    dma = pltpu.SemaphoreType.DMA
    kind = jnp.bfloat16
    pairs = dma((2, chunks))
    return pl.pallas_call(
        functools.partial(gather_kernel, count, chunks),
        out_shape=jax.ShapeDtypeStruct((count, rows // count, cols), kind),
        in_specs=[pl.BlockSpec(memory_space=pltpu.VMEM)] * 5,
        out_specs=pl.BlockSpec(memory_space=pl.ANY),
        scratch_shapes=[
            pltpu.VMEM((4, rows, cols), kind),
            pltpu.VMEM((rows, half), kind),
            pltpu.VMEM((rows, cols - half), kind),
            pltpu.VMEM((rows, cols), kind),
            pltpu.VMEM((rows, cols), kind),
            pltpu.VMEM((count, rows // count, cols), kind),
            pairs,
            pairs,
            pairs,
            pairs,
            pairs,
            pairs,
            dma((count,)),
            dma((count,)),
            dma((1,)),
        ],
        compiler_params=pltpu.CompilerParams(
            collective_id=1, has_side_effects=True, vmem_limit_bytes=VMEM_LIMIT
        ),
        name="gather",
    )(gg, gu, score, gate_w, up_w)


def fused_kernel(
    count, sent_in, sent_dy, gate_w, up_w, down_w,
    all_in, all_dy, back, grad_gate, grad_up, grad_down,
    stage, flat_in, flat_dy, hid, dgate, dup, part, far_l, far_r, near_l, near_r, zed, total,
    z_s, z_r, side_s, side_r, far_s, far_r_sem, own_sem, stage_sem,
    rf_s, rf_r, rd_s, rd_r, rs_s, rs_r, home_s, home_r,
):
    own_e = lax.axis_index("expert")
    own_d, right, left = ring_places()
    sent, full, flat = (sent_in, sent_dy), (all_in, all_dy), (flat_in, flat_dy)
    sides = (right, left)
    dp_count, _, cap, width = all_in.shape
    cols = part.shape[3]
    group = dp_count * cap
    half = width // 2
    halves = (pl.ds(0, half), pl.ds(half, cols - half))
    spans = ((0, half), (half, cols))
    far_in, near_in = (far_l, far_r), (near_l, near_r)
    tile = 512
    last_dims = (((1,), (1,)), ((), ()))
    first_dims = (((0,), (0,)), ((), ()))

    def z_copy(a, i):
        peer = partner(own_e, i, count)
        return remote(
            sent[a].at[peer], full[a].at[own_d, own_e], z_s.at[a, i], z_r.at[a, i], "expert", peer
        )

    def z_landed(a, i):
        place = full[a].at[own_d, partner(own_e, i, count)]
        return remote(place, place, z_s.at[a, i], z_r.at[a, i], "expert", own_e)

    def side_copy(a, way, i, src=None):
        place = full[a].at[own_d, partner(own_e, i, count)]
        return remote(
            place if src is None else src, place, side_s.at[a, way, i], side_r.at[a, way, i], "dp", sides[way]
        )

    def side_landed(a, way, i):
        place = full[a].at[sides[1 - way], partner(own_e, i, count)]
        return remote(place, place, side_s.at[a, way, i], side_r.at[a, way, i], "dp", sides[way])

    def onward_copy(a, i):
        place = full[a].at[sides[1 - a], partner(own_e, i, count)]
        return remote(place, place, far_s.at[a, i], far_r_sem.at[a, i], "dp", sides[a])

    def onward_landed(a, i):
        place = full[a].at[3 - own_d, partner(own_e, i, count)]
        return remote(place, place, far_s.at[a, i], far_r_sem.at[a, i], "dp", sides[a])

    def rf_copy(way, c):
        return remote(
            part.at[3 - own_d, c, :, halves[way]], far_in[way].at[c],
            rf_s.at[way, c], rf_r.at[way, c], "dp", sides[way],
        )

    def rd_copy(way, c):
        return remote(
            part.at[sides[way], c, :, halves[1 - way]], near_in[way].at[c, :, halves[1 - way]],
            rd_s.at[way, c], rd_r.at[way, c], "dp", sides[way],
        )

    def rs_copy(way, c):
        return remote(
            part.at[sides[way], c, :, halves[way]], near_in[way].at[c, :, halves[way]],
            rs_s.at[way, c], rs_r.at[way, c], "dp", sides[way],
        )

    def home_copy(i):
        peer = partner(own_e, i, count)
        return remote(zed.at[i], back.at[own_e], home_s.at[i], home_r.at[i], "expert", peer)

    def home_landed(i):
        place = back.at[partner(own_e, i, count)]
        return remote(place, place, home_s.at[i], home_r.at[i], "expert", own_e)

    own = [
        pltpu.make_async_copy(sent[a].at[own_e], full[a].at[own_d, own_e], own_sem.at[a])
        for a in range(2)
    ]
    for a in range(2):
        own[a].start()
    greet(count, own_e, right, left)
    for a in range(2):
        for way in range(2):
            side_copy(a, way, 0, sent[a].at[own_e]).start()

    def start(i, carry):
        for a in range(2):
            z_copy(a, i).start()
        return carry

    lax.fori_loop(1, min(4, count), start, 0)
    for a in range(2):
        own[a].wait()

    def relay(i):
        for a in range(2):
            z_landed(a, i).wait_recv()
            for way in range(2):
                side_copy(a, way, i).start()

        @pl.when(i + 3 < count)
        def _():
            start(i + 3, 0)

    def onward(i):
        for a in range(2):
            side_landed(a, a, i).wait_recv()
            onward_copy(a, i).start()

    def compute(i):
        src = partner(own_e, i, count)
        for a in range(2):
            side_landed(a, 1 - a, i).wait_recv()
            onward_landed(a, i).wait_recv()
        loads = [
            pltpu.make_async_copy(full[a].at[:, src], stage.at[a], stage_sem.at[a])
            for a in range(2)
        ]
        for load in loads:
            load.start()
        for load in loads:
            load.wait()
        rows = pl.ds(pl.multiple_of(i * group, group), group)
        for a in range(2):
            for at in col_tiles(0, width, tile):
                value = stage[a, :, :, at].astype(jnp.float32).reshape(group, tile)
                flat[a][rows, at] = value.astype(flat[a].dtype)

        def product(x, w):
            return lax.dot_general(x, w, last_dims, preferred_element_type=jnp.float32)

        gate_pre = product(flat_in[rows, :], gate_w[...])
        up_pre = product(flat_in[rows, :], up_w[...])
        back_hidden = product(flat_dy[rows, :], down_w[...])
        sigmoid_gate = jax.nn.sigmoid(gate_pre)
        active = gate_pre * sigmoid_gate
        hidden = (active * up_pre).astype(jnp.bfloat16)
        score = jnp.sum(back_hidden * hidden.astype(jnp.float32), axis=1, keepdims=True)
        g = (back_hidden * up_pre * sigmoid_gate * (1.0 + gate_pre * (1.0 - sigmoid_gate))).astype(
            jnp.bfloat16
        )
        u = (back_hidden * active).astype(jnp.bfloat16)
        hid[rows, :] = hidden
        dgate[rows, :] = g
        dup[rows, :] = u
        score = jnp.broadcast_to(score, (group, cols - width)).reshape(dp_count, cap, cols - width)
        part[:, i, :, width:cols] = score.astype(part.dtype)
        for at in col_tiles(0, width, tile):
            value = jnp.dot(g, gate_w[:, at], preferred_element_type=jnp.float32)
            value = value + jnp.dot(u, up_w[:, at], preferred_element_type=jnp.float32)
            part[:, i, :, at] = value.reshape(dp_count, cap, tile).astype(part.dtype)
        for way in range(2):
            rf_copy(way, i).start()
        for way in range(2):
            rd_copy(way, i).start()

    def ring_sum(i):
        for way in range(2):
            rf_copy(way, i).wait_recv()
            for at in col_tiles(*spans[way], tile):
                there = slice(at.start - spans[way][0], at.stop - spans[way][0])
                summed = part[sides[way], i, :, at].astype(jnp.float32)
                summed = summed + far_in[way][i, :, there].astype(jnp.float32)
                part[sides[way], i, :, at] = summed.astype(part.dtype)
            rs_copy(way, i).start()

    def merge(i):
        for way in range(2):
            rd_copy(way, i).wait_recv()
            rs_copy(way, i).wait_recv()
        for at in col_tiles(0, cols, tile):
            summed = part[own_d, i, :, at].astype(jnp.float32)
            summed = summed + near_l[i, :, at].astype(jnp.float32)
            summed = summed + near_r[i, :, at].astype(jnp.float32)
            zed[i, :, at] = summed.astype(zed.dtype)

        @pl.when(i > 0)
        def _():
            home_copy(i).start()

    def weight_grad(k, out, left_rows, right_rows, pair):
        rows = pl.ds(pl.multiple_of(pair * 2 * group, 2 * group), 2 * group)
        left_part = left_rows[rows, :]

        def one(j, carry):
            at = pl.ds(pl.multiple_of(j * tile, tile), tile)
            value = lax.dot_general(
                left_part, right_rows[rows, at], first_dims, preferred_element_type=jnp.float32
            )

            @pl.when(pair == 0)
            def _():
                total[k, :, at] = value

            @pl.when((pair > 0) & (pair < count // 2 - 1))
            def _():
                total[k, :, at] += value

            @pl.when(pair == count // 2 - 1)
            def _():
                out[:, at] = (total[k, :, at] + value).astype(out.dtype)

            return carry

        lax.fori_loop(0, width // tile, one, 0)

    grads = ((grad_down, hid, flat_dy), (grad_gate, dgate, flat_in), (grad_up, dup, flat_in))

    def step(t, carry):
        def during(lag, first, f):
            @pl.when((t - lag >= first) & (t - lag < count))
            def _():
                f(t - lag)

        during(0, 1, relay)
        during(1, 0, onward)
        during(3, 0, ring_sum)
        during(2, 0, compute)
        during(4, 0, merge)

        @pl.when((t >= 4) & (t < count + 4) & (t % 2 == 0))
        def _():
            for k, grad in enumerate(grads):
                weight_grad(k, *grad, (t - 4) // 2)

        return carry

    lax.fori_loop(0, count + 4, step, 0)
    keep = pltpu.make_async_copy(zed.at[0], back.at[own_e], own_sem.at[0])
    keep.start()
    keep.wait()

    def finish(i, carry):
        for a in range(2):
            onward_copy(a, i).wait_send()
            for way in range(2):
                side_copy(a, way, i).wait_send()
        for way in range(2):
            rf_copy(way, i).wait_send()
            rd_copy(way, i).wait_send()
            rs_copy(way, i).wait_send()
        return carry

    lax.fori_loop(0, count, finish, 0)

    def landed(i, carry):
        for a in range(2):
            z_copy(a, i).wait_send()
        home_landed(i).wait_recv()
        home_copy(i).wait_send()
        return carry

    lax.fori_loop(1, count, landed, 0)


def fused(sent_in, sent_dy, gate_t, up_t, down_w, dp_count):
    count, cap, width = sent_in.shape
    kind = sent_in.dtype
    hidden = down_w.shape[0]
    cols, half = width + LANES, width // 2
    row_count = dp_count * count * cap
    dma = pltpu.SemaphoreType.DMA
    full = jax.ShapeDtypeStruct((dp_count, count, cap, width), kind)
    grad = jax.ShapeDtypeStruct((hidden, width), kind)
    whole = pl.BlockSpec(memory_space=pltpu.VMEM)
    apart = pl.BlockSpec(memory_space=pl.ANY)
    pair = dma((2, count))
    results = pl.pallas_call(
        functools.partial(fused_kernel, count),
        out_shape=(full, full, jax.ShapeDtypeStruct((count, cap, cols), kind), grad, grad, grad),
        in_specs=[apart, apart, whole, whole, whole],
        out_specs=[apart, apart, apart, whole, whole, whole],
        scratch_shapes=[
            pltpu.VMEM((2, dp_count, cap, width), kind),
            pltpu.VMEM((row_count, width), kind),
            pltpu.VMEM((row_count, width), kind),
            pltpu.VMEM((row_count, hidden), kind),
            pltpu.VMEM((row_count, hidden), kind),
            pltpu.VMEM((row_count, hidden), kind),
            pltpu.VMEM((dp_count, count, cap, cols), kind),
            pltpu.VMEM((count, cap, half), kind),
            pltpu.VMEM((count, cap, cols - half), kind),
            pltpu.VMEM((count, cap, cols), kind),
            pltpu.VMEM((count, cap, cols), kind),
            pltpu.VMEM((count, cap, cols), kind),
            pltpu.VMEM((3, hidden, width), jnp.float32),
            pair,
            pair,
            dma((2, 2, count)),
            dma((2, 2, count)),
            pair,
            pair,
            dma((2,)),
            dma((2,)),
            pair,
            pair,
            pair,
            pair,
            pair,
            pair,
            dma((count,)),
            dma((count,)),
        ],
        compiler_params=pltpu.CompilerParams(
            collective_id=2, has_side_effects=True, vmem_limit_bytes=VMEM_LIMIT
        ),
        name="fused",
    )(sent_in, sent_dy, gate_t, up_t, down_w)
    return results[2:]


def body(tokens, out_grad, routes, gate_probs, w_gate, w_up, w_down):
    expert_count = lax.axis_size("expert")
    dp_count = lax.axis_size("dp")
    tok_count, width = tokens.shape
    top_count = routes.shape[1]
    capacity = 3 * tok_count * top_count // (2 * expert_count)
    capacity = -(-capacity // 8) * 8
    slot_total = expert_count * capacity
    flat_routes = routes.reshape(-1)
    order = jnp.arange(flat_routes.shape[0], dtype=jnp.int32)
    same = (flat_routes[:, None] == flat_routes[None, :]) & (order[None, :] < order[:, None])
    slot_index = jnp.sum(same.astype(jnp.int32), axis=1)
    destination = flat_routes * capacity + slot_index
    placing = jnp.arange(slot_total, dtype=jnp.int32)[:, None] == destination[None, :]
    weights = gate_probs.reshape(-1).astype(jnp.float32)
    by_token = placing.astype(jnp.bfloat16).reshape(slot_total, tok_count, top_count)
    collect = jnp.sum(by_token, axis=2)
    weighted = jnp.where(placing, weights[None, :], 0.0).astype(jnp.bfloat16)
    collect_weighted = jnp.sum(weighted.reshape(slot_total, tok_count, top_count), axis=2)
    sent_shape = (expert_count, capacity, width)
    sent_in = (
        jnp.dot(collect, tokens, preferred_element_type=jnp.float32)
        .astype(jnp.bfloat16)
        .reshape(sent_shape)
    )
    sent_dy = (
        jnp.dot(collect_weighted, out_grad, preferred_element_type=jnp.float32)
        .astype(jnp.bfloat16)
        .reshape(sent_shape)
    )
    contract_first = (((0,), (0,)), ((), ()))
    row_total = dp_count * slot_total
    if row_total <= 1024 and expert_count % 2 == 0 and (dp_count * capacity) % 16 == 0:
        back, grad_gate, grad_up, grad_down = fused(
            sent_in, sent_dy, w_gate[0].T, w_up[0].T, w_down[0], dp_count
        )
        grad_gate, grad_up = grad_gate.T, grad_up.T
    else:
        all_in, all_dy = spread(sent_in, sent_dy, dp_count)
        rows_in = all_in.reshape(row_total, width)
        scaled = all_dy.reshape(row_total, width)
        gate_w = w_gate[0]
        up_w = w_up[0]
        down_w = w_down[0]
        contract_last = (((1,), (1,)), ((), ()))
        gate_pre = jnp.dot(rows_in, gate_w, preferred_element_type=jnp.float32)
        up_pre = jnp.dot(rows_in, up_w, preferred_element_type=jnp.float32)
        sigmoid_gate = jax.nn.sigmoid(gate_pre)
        active = gate_pre * sigmoid_gate
        hidden = (active * up_pre).astype(jnp.bfloat16)
        back_hidden = lax.dot_general(scaled, down_w, contract_last, preferred_element_type=jnp.float32)
        grad_gate_pre = (
            back_hidden * up_pre * sigmoid_gate * (1.0 + gate_pre * (1.0 - sigmoid_gate))
        ).astype(jnp.bfloat16)
        grad_up_pre = (back_hidden * active).astype(jnp.bfloat16)
        score = jnp.sum(back_hidden * hidden.astype(jnp.float32), axis=1, keepdims=True)
        score = jnp.broadcast_to(score, (row_total, LANES)).astype(jnp.bfloat16)
        back = gather(grad_gate_pre, grad_up_pre, score, gate_w, up_w, expert_count, dp_count)
        grad_down = lax.dot_general(
            hidden, scaled, contract_first, preferred_element_type=jnp.float32
        ).astype(jnp.bfloat16)
        grad_gate = lax.dot_general(
            rows_in, grad_gate_pre, contract_first, preferred_element_type=jnp.float32
        ).astype(jnp.bfloat16)
        grad_up = lax.dot_general(
            rows_in, grad_up_pre, contract_first, preferred_element_type=jnp.float32
        ).astype(jnp.bfloat16)
    back = back.reshape(slot_total, width + LANES)
    grad_tokens = lax.dot_general(
        collect, back[:, :width], contract_first, preferred_element_type=jnp.float32
    ).astype(jnp.bfloat16)
    picked = lax.dot_general(
        placing.astype(jnp.bfloat16),
        back[:, width:],
        contract_first,
        preferred_element_type=jnp.float32,
    )[:, 0]
    grad_probs = (picked / weights).astype(jnp.bfloat16).reshape(tok_count, top_count)
    return (grad_tokens, grad_probs, grad_gate[None], grad_up[None], grad_down[None])


def solution(mesh):
    in_specs = (
        P(("dp", "expert"), None),
        P(("dp", "expert"), None),
        P(("dp", "expert"), None),
        P(("dp", "expert"), None),
        P("expert", None, "dp"),
        P("expert", None, "dp"),
        P("expert", "dp", None),
    )
    out_specs = (
        P(("dp", "expert"), None),
        P(("dp", "expert"), None),
        P("expert", None, "dp"),
        P("expert", None, "dp"),
        P("expert", "dp", None),
    )
    return jax.shard_map(body, mesh=mesh, in_specs=in_specs, out_specs=out_specs, check_vma=False)
```
